128 devices in a mesh: view: 4 (over x), pix: 32 (over y, z, core).
Axes of the slice: x: 4, y: 4, z: 4, core: 2. Of those that a mesh axis runs over, the one named last changes fastest.
Arguments:
- centers: float32 [3, 1048576], P(None, ('view', 'pix'))
- log_scales: float32 [3, 1048576], P(None, ('view', 'pix')), may hold values from -4.8 to -3.5
- rotations: float32 [4, 1048576], P(None, ('view', 'pix')), may hold values from 0.3 to 1.5
- logits: float32 [1048576], P(('view', 'pix')), may hold values from -7 to -4
- harmonic_coeffs: float32 [48, 1048576], P(None, ('view', 'pix')), may hold values from -3 to 3
- cameras: float32 [4, 6], replicated, may hold values from -0.004 to 0.004
- send_ids: int32 [128, 32, 256], P(('view', 'pix')), may hold values from -1 to 8191, as said below
- tile_lists: int32 [512, 2048], P('pix'), may hold values from -1 to 32767, as said below
- tile_perm: int32 [512], P('pix'), may hold values from 0 to 511, as said below
- targets: float32 [4, 512, 3, 256], P('view', 'pix'), may hold values from 0 to 1
Outputs:
- rendered: float32 [4, 512, 3, 256], P('view', 'pix')
- total_loss: float32 [], replicated
- grad_centers: float32 [3, 1048576], P(None, ('view', 'pix'))
- grad_scales: float32 [3, 1048576], P(None, ('view', 'pix'))
- grad_rotations: float32 [4, 1048576], P(None, ('view', 'pix'))
- grad_logits: float32 [1048576], P(('view', 'pix'))
- grad_harmonics: float32 [48, 1048576], P(None, ('view', 'pix'))
The draws below stay inside these ranges and needn't reach their ends.
Inputs may be any that keep to these rules, and one draw needn't show every extreme that they name: `send_ids`: entry [s, p, c] is a local index of device s's Gaussians or -1; the indices of one device are distinct. `tile_lists`: in each row the listed receive slots come first, distinct, ordered front to back, then -1; a listed slot e of row r has send_ids[e // 256, r // 16, e % 256] >= 0 and (e % 256) // 16 == r % 16; some row has all 2048 entries. `tile_perm`: A permutation of the tiles of a view.
All inputs are finite; a program needn't handle non-finite values.
Results may differ from the reference program's by a relative error of at most 0.0003.
Values sent between devices are 32-bit elements; how exact they have to be, the bound alone decides.
A program may use at most 192 MiB of HBM per device.

```python
import jax
import jax.numpy as jnp
from jax import lax

TILES_DEV = 16
PER = 16
TW = 16
SH = 48
VIEWS = 4
TILES = 512
CAP = 256
K = 2048
G_DEV = 8192
GAUSS = 1048576
DEVICES = 128


FOCAL = 1100.0


def layout(key):
    subkeys = jax.random.split(key, 5)
    tile_order = jax.random.permutation(subkeys[0], TILES).astype(jnp.int32)
    candidate = jax.vmap(lambda single: jax.random.permutation(single, K))(jax.random.split(subkeys[1], TILES)).astype(jnp.int32)
    raw_draw = jax.random.randint(subkeys[2], (TILES,), 1, K + 1)
    length = jnp.maximum(1, (raw_draw * raw_draw // K + raw_draw) // 2)
    full_row = jax.random.randint(subkeys[3], (), 0, TILES)
    length = jnp.where(jnp.arange(TILES) == full_row, K, length).astype(jnp.int32)
    slot_owner = jax.vmap(lambda single: jax.random.permutation(single, G_DEV))(jax.random.split(subkeys[4], DEVICES)).astype(jnp.int32)
    position_rank = jnp.argsort(candidate, axis=1).astype(jnp.int32)
    return (tile_order, candidate, length, slot_owner, position_rank)


def draw_tile_perm(key, part):
    tile_order, candidate, length, slot_owner, position_rank = layout(key)
    return tile_order


def draw_tile_lists(key, part):
    tile_order, candidate, length, slot_owner, position_rank = layout(key)
    column = jnp.arange(K, dtype=jnp.int32)[None, :]
    source = candidate // PER
    slot_index = (jnp.arange(TILES, dtype=jnp.int32) % TILES_DEV)[:, None] * PER + candidate % PER
    listed = source * CAP + slot_index
    return jnp.where(column < length[:, None], listed, -1).astype(jnp.int32)


def draw_send_ids(key, part):
    tile_order, candidate, length, slot_owner, position_rank = layout(key)
    source = jnp.arange(DEVICES, dtype=jnp.int32)[:, None, None]
    owner_pix = jnp.arange(TILES // TILES_DEV, dtype=jnp.int32)[None, :, None]
    slot_index = jnp.arange(CAP, dtype=jnp.int32)[None, None, :]
    row_index = owner_pix * TILES_DEV + slot_index // PER
    chosen = source * PER + slot_index % PER
    used = position_rank[row_index, chosen] < length[row_index]
    local_ids = slot_owner[source, owner_pix * CAP + slot_index]
    return jnp.where(used, local_ids, -1).astype(jnp.int32)


def draw_centers(key, part):
    tile_order, candidate, length, slot_owner, position_rank = layout(key)
    key = jax.random.fold_in(key, 4)
    inverse = jnp.argsort(slot_owner, axis=1).astype(jnp.int32)
    source = jnp.arange(DEVICES, dtype=jnp.int32)[:, None]
    owner_pix = inverse // CAP
    slot_index = inverse % CAP
    row_index = owner_pix * TILES_DEV + slot_index // PER
    chosen = source * PER + slot_index % PER
    position = position_rank[row_index, chosen].astype(jnp.float32)
    tile_index = tile_order[row_index]
    noise = jax.random.uniform(key, (3, DEVICES, G_DEV), jnp.float32)
    depth = 4.0 + 2.0 * (position + 0.5 * noise[2]) / K
    screen_x = (16 * (tile_index % TW)).astype(jnp.float32) + 2.0 + 12.0 * noise[0]
    screen_y = (16 * (tile_index // TW)).astype(jnp.float32) + 2.0 + 12.0 * noise[1]
    world_x = (screen_x - 8.0 * TW) * depth / FOCAL
    world_y = (screen_y - 8.0 * (TILES // TW)) * depth / FOCAL
    return jnp.stack([world_x, world_y, depth]).reshape(3, GAUSS)


def levels(key, dims, pieces, least, top_value):
    level, own = 1.0, jax.random.fold_in(key, 6)
    for dim, blocks in pieces:
        heights = jnp.exp(jax.random.uniform(jax.random.fold_in(own, dim), (blocks,), jnp.float32, least / len(pieces), top_value / len(pieces)))
        level = level * jnp.repeat(heights, dims[dim] // blocks).reshape([-1 if axis == dim else 1 for axis in range(len(dims))])
    return level


def scatter_about(stream_key, shape, deviation, reach, cuts=(), held_as=jnp.bfloat16):
    result = jax.random.normal(stream_key, shape, jnp.float32) * deviation
    if len(cuts) > 0:
        result = levels(stream_key, shape, cuts, -0.22, 0.18) * result
    return jnp.clip(result, min=-reach, max=reach).astype(held_as)


def setup_inputs(seed: int = 0) -> dict:
    splits = jax.random.split(jax.random.key(seed), 11)
    return {
        "centers": draw_centers(jax.random.fold_in(splits[10], 71), 0),
        "log_scales": jnp.clip(-4.8 + 1.3000002 * jax.random.uniform(splits[1], (3, GAUSS), jnp.float32) ** levels(splits[1], (3, GAUSS), ((1, 128),), -0.2, 0.2), -4.8, -3.5),
        "rotations": jnp.clip(0.3 + 1.2 * jax.random.uniform(splits[2], (4, GAUSS), jnp.float32) ** levels(splits[2], (4, GAUSS), ((1, 128),), -0.2, 0.2), 0.3, 1.5),
        "logits": jnp.clip(-7.0 + 3.0 * jax.random.uniform(splits[3], (GAUSS,), jnp.float32) ** levels(splits[3], (GAUSS,), ((0, 128),), -0.2, 0.2), -7.0, -4.0),
        "harmonic_coeffs": scatter_about(splits[4], (SH, GAUSS), 0.5, 3.0, ((1, 128),), jnp.float32),
        "cameras": jnp.clip(jax.random.uniform(splits[5], (VIEWS, 6), jnp.float32, -0.004, 0.004), -0.004, 0.004),
        "send_ids": draw_send_ids(jax.random.fold_in(splits[10], 71), 0),
        "tile_lists": draw_tile_lists(jax.random.fold_in(splits[10], 71), 0),
        "tile_perm": draw_tile_perm(jax.random.fold_in(splits[10], 71), 0),
        "targets": jnp.clip(1.0 * jax.random.uniform(splits[9], (VIEWS, TILES, 3, 256), jnp.float32) ** levels(splits[9], (VIEWS, TILES, 3, 256), ((0, 4), (1, 32)), -0.2, 0.2), 0.0, 1.0),
    }


FOCAL = 1100.0
BLUR = 0.3
SH_ZERO = 0.28209479177387814
SH_ONE = 0.4886025119029199
SH_TWO = (1.0925484305920792, -1.0925484305920792, 0.31539156525252005, -1.0925484305920792, 0.5462742152960396)
SH_THREE = (-0.5900435899266435, 2.890611442640554, -0.4570457994644658, 0.3731763325901154, -0.4570457994644658, 1.445305721320277, -0.5900435899266435)

def rotation_matrix(camera):
    cos_a, cos_b, cos_c = (jnp.cos(camera[0]), jnp.cos(camera[1]), jnp.cos(camera[2]))
    sin_a, sin_b, sin_c = (jnp.sin(camera[0]), jnp.sin(camera[1]), jnp.sin(camera[2]))
    return [[cos_c * cos_b, cos_c * sin_b * sin_a - sin_c * cos_a, cos_c * sin_b * cos_a + sin_c * sin_a], [sin_c * cos_b, sin_c * sin_b * sin_a + cos_c * cos_a, sin_c * sin_b * cos_a - cos_c * sin_a], [-sin_b, cos_b * sin_a, cos_b * cos_a]]

def harmonics(direction):
    dir_x, dir_y, dir_z = (direction[0], direction[1], direction[2])
    sq_x, sq_y, sq_z = (dir_x * dir_x, dir_y * dir_y, dir_z * dir_z)
    terms = [SH_ZERO * jnp.ones_like(dir_x), -SH_ONE * dir_y, SH_ONE * dir_z, -SH_ONE * dir_x, SH_TWO[0] * dir_x * dir_y, SH_TWO[1] * dir_y * dir_z, SH_TWO[2] * (2.0 * sq_z - sq_x - sq_y), SH_TWO[3] * dir_x * dir_z, SH_TWO[4] * (sq_x - sq_y), SH_THREE[0] * dir_y * (3.0 * sq_x - sq_y), SH_THREE[1] * dir_x * dir_y * dir_z, SH_THREE[2] * dir_y * (4.0 * sq_z - sq_x - sq_y), SH_THREE[3] * dir_z * (2.0 * sq_z - 3.0 * sq_x - 3.0 * sq_y), SH_THREE[4] * dir_x * (4.0 * sq_z - sq_x - sq_y), SH_THREE[5] * dir_z * (sq_x - sq_y), SH_THREE[6] * dir_x * (sq_x - 3.0 * sq_y)]
    return jnp.stack(terms)

def project(centers, log_scales, rotations, logits, harmonic_coeffs, camera, width_px, height_px):
    turn = rotation_matrix(camera)
    camera_pts = [sum((turn[line_idx][entry_idx] * centers[entry_idx] for entry_idx in range(3))) + camera[3 + line_idx] for line_idx in range(3)]
    cam_x, cam_y, depth = camera_pts
    length_q = jnp.sqrt(lax.optimization_barrier(jnp.sum(rotations * rotations, axis=0)))
    unit = rotations / length_q[None, :]
    scalar_part, vector_x, vector_y, vector_z = (unit[0], unit[1], unit[2], unit[3])
    quat_turn = [[1.0 - 2.0 * (vector_y * vector_y + vector_z * vector_z), 2.0 * (vector_x * vector_y - scalar_part * vector_z), 2.0 * (vector_x * vector_z + scalar_part * vector_y)], [2.0 * (vector_x * vector_y + scalar_part * vector_z), 1.0 - 2.0 * (vector_x * vector_x + vector_z * vector_z), 2.0 * (vector_y * vector_z - scalar_part * vector_x)], [2.0 * (vector_x * vector_z - scalar_part * vector_y), 2.0 * (vector_y * vector_z + scalar_part * vector_x), 1.0 - 2.0 * (vector_x * vector_x + vector_y * vector_y)]]
    spread = jnp.exp(log_scales)
    shaped = [[quat_turn[line_idx][entry_idx] * spread[entry_idx] for entry_idx in range(3)] for line_idx in range(3)]
    sigma = [[sum((shaped[line_idx][inner_idx] * shaped[entry_idx][inner_idx] for inner_idx in range(3))) for entry_idx in range(3)] for line_idx in range(3)]
    inverse_depth = 1.0 / depth
    jac_diag = FOCAL * inverse_depth
    jac_x = -FOCAL * cam_x * inverse_depth * inverse_depth
    jac_y = -FOCAL * cam_y * inverse_depth * inverse_depth
    first_row = [jac_diag * turn[0][entry_idx] + jac_x * turn[2][entry_idx] for entry_idx in range(3)]
    second_row = [jac_diag * turn[1][entry_idx] + jac_y * turn[2][entry_idx] for entry_idx in range(3)]

    def quadratic(left_row, right_row):
        return sum((left_row[line_idx] * sigma[line_idx][entry_idx] * right_row[entry_idx] for line_idx in range(3) for entry_idx in range(3)))
    cov_xx = quadratic(first_row, first_row) + BLUR
    cov_xy = quadratic(first_row, second_row)
    cov_yy = quadratic(second_row, second_row) + BLUR
    determinant = cov_xx * cov_yy - cov_xy * cov_xy
    screen_x = FOCAL * cam_x * inverse_depth + 0.5 * width_px
    screen_y = FOCAL * cam_y * inverse_depth + 0.5 * height_px
    opacity = jax.nn.sigmoid(logits)
    anchor = [-sum((turn[line_idx][entry_idx] * camera[3 + line_idx] for line_idx in range(3))) for entry_idx in range(3)]
    offsets = jnp.stack([centers[entry_idx] - anchor[entry_idx] for entry_idx in range(3)])
    direction = offsets / jnp.sqrt(lax.optimization_barrier(jnp.sum(offsets * offsets, axis=0)))[None, :]
    basis = harmonics(direction)
    colour = jnp.maximum(lax.optimization_barrier(jnp.sum(harmonic_coeffs.reshape(3, 16, -1) * basis[None], axis=1)) + 0.5, 0.0)
    return jnp.stack([screen_x, screen_y, cov_yy / determinant, -cov_xy / determinant, cov_xx / determinant, opacity, colour[0], colour[1], colour[2]])

def alpha_of(record, pixel_x, pixel_y):
    delta_x = pixel_x[:, None] - record[0][None, :]
    delta_y = pixel_y[:, None] - record[1][None, :]
    exponent = -0.5 * (record[2][None, :] * delta_x * delta_x + record[4][None, :] * delta_y * delta_y) - record[3][None, :] * delta_x * delta_y
    return record[5][None, :] * jnp.exp(exponent)

def render_tile(record, pixel_x, pixel_y):
    alphas = alpha_of(record, pixel_x, pixel_y)
    log_keep = jnp.log(1.0 - alphas)
    transmit = jnp.exp(jnp.cumsum(log_keep, axis=1) - log_keep)
    weights = alphas * transmit
    return jnp.dot(record[6:9], weights.T, precision=lax.Precision.HIGHEST)

def reference(centers, log_scales, rotations, logits, harmonic_coeffs, cameras, send_ids, tile_lists, tile_perm, targets):
    width_px = 16 * TW
    height_px = 16 * (TILES // TW)
    valid = tile_lists >= 0
    entries = jnp.where(valid, tile_lists, 0).astype(jnp.int32)
    source = (entries // CAP).astype(jnp.int32)
    owner_pix = (jnp.arange(TILES, dtype=jnp.int32) // TILES_DEV)[:, None]
    local_ids = send_ids[source, owner_pix, entries % CAP]
    global_ids = jnp.where(valid, source * G_DEV + local_ids, 0).astype(jnp.int32)
    mask = valid.astype(jnp.float32)
    offsets = jnp.arange(256, dtype=jnp.int32)
    pixel_x = (16 * (tile_perm % TW))[:, None] + (offsets % 16)[None, :]
    pixel_y = (16 * (tile_perm // TW))[:, None] + (offsets // 16)[None, :]
    pixel_x = pixel_x.astype(jnp.float32)
    pixel_y = pixel_y.astype(jnp.float32)
    render_saved = jax.checkpoint(render_tile)

    def objective(params):
        frames = []
        for view_idx in range(VIEWS):
            record = project(params[0], params[1], params[2], params[3], params[4], cameras[view_idx], width_px, height_px)
            picked = jnp.transpose(record[:, global_ids], (1, 0, 2)) * mask[:, None, :]
            frames.append(lax.map(lambda packed: render_saved(packed[0], packed[1], packed[2]), (picked, pixel_x, pixel_y)))
        rendered = jnp.stack(frames)
        residual = rendered - targets
        return (0.5 * jnp.sum(residual * residual), rendered)
    (total_loss, rendered), grads = jax.value_and_grad(objective, has_aux=True)((centers, log_scales, rotations, logits, harmonic_coeffs))
    return (rendered, total_loss, grads[0], grads[1], grads[2], grads[3], grads[4])
```

```python
import functools

import jax
import jax.numpy as jnp
from jax import lax
from jax.experimental import pallas as pl
from jax.experimental.pallas import tpu as pltpu
from jax.sharding import PartitionSpec as P

TW = 16
FOCAL = 1100.0
BLUR = 0.3
SH_ZERO = 0.28209479177387814
SH_ONE = 0.4886025119029199
SH_TWO = (
    1.0925484305920792,
    -1.0925484305920792,
    0.31539156525252005,
    -1.0925484305920792,
    0.5462742152960396,
)
SH_THREE = (
    -0.5900435899266435,
    2.890611442640554,
    -0.4570457994644658,
    0.3731763325901154,
    -0.4570457994644658,
    1.445305721320277,
    -0.5900435899266435,
)
LOG2E = 1.4426950408889634
LANES = 128
VIEWS = 4
FIELDS = 9
MSG = 24
TBL = 40
BLOCKS = 64
F32 = jnp.float32
I32 = jnp.int32
BF16 = jnp.bfloat16


def camera_numbers(cameras):
    cos, sin = jnp.cos(cameras[:, :3]), jnp.sin(cameras[:, :3])
    ca, cb, cc = cos[:, 0], cos[:, 1], cos[:, 2]
    sa, sb, sc = sin[:, 0], sin[:, 1], sin[:, 2]
    turn = [
        [cc * cb, cc * sb * sa - sc * ca, cc * sb * ca + sc * sa],
        [sc * cb, sc * sb * sa + cc * ca, sc * sb * ca - cc * sa],
        [-sb, cb * sa, cb * ca],
    ]
    shift = [cameras[:, 3], cameras[:, 4], cameras[:, 5]]
    anchor = [-sum(turn[i][e] * shift[i] for i in range(3)) for e in range(3)]
    return jnp.stack(turn[0] + turn[1] + turn[2] + shift + anchor + [shift[0]], axis=1)


def harmonics(x, y, z):
    xx, yy, zz = x * x, y * y, z * z
    return [
        SH_ZERO * jnp.ones_like(x),
        -SH_ONE * y,
        SH_ONE * z,
        -SH_ONE * x,
        SH_TWO[0] * x * y,
        SH_TWO[1] * y * z,
        SH_TWO[2] * (2.0 * zz - xx - yy),
        SH_TWO[3] * x * z,
        SH_TWO[4] * (xx - yy),
        SH_THREE[0] * y * (3.0 * xx - yy),
        SH_THREE[1] * x * y * z,
        SH_THREE[2] * y * (4.0 * zz - xx - yy),
        SH_THREE[3] * z * (2.0 * zz - 3.0 * xx - 3.0 * yy),
        SH_THREE[4] * x * (4.0 * zz - xx - yy),
        SH_THREE[5] * z * (xx - yy),
        SH_THREE[6] * x * (xx - 3.0 * yy),
    ]


def shape_of(scales, rots):
    inv = 1.0 / jnp.sqrt(sum(q * q for q in rots))
    s, x, y, z = [q * inv for q in rots]
    turn = [
        [1.0 - 2.0 * (y * y + z * z), 2.0 * (x * y - s * z), 2.0 * (x * z + s * y)],
        [2.0 * (x * y + s * z), 1.0 - 2.0 * (x * x + z * z), 2.0 * (y * z - s * x)],
        [2.0 * (x * z - s * y), 2.0 * (y * z + s * x), 1.0 - 2.0 * (x * x + y * y)],
    ]
    spread = [jnp.exp(v) for v in scales]
    m = [[turn[i][e] * spread[e] for e in range(3)] for i in range(3)]
    pairs = ((0, 0), (0, 1), (0, 2), (1, 1), (1, 2), (2, 2))
    return [sum(m[i][e] * m[k][e] for e in range(3)) for i, k in pairs]


def geometry(centers, sigma, cam, width_px, height_px):
    pts = [
        sum(cam[3 * i + e] * centers[e] for e in range(3)) + cam[9 + i] for i in range(3)
    ]
    inv = 1.0 / pts[2]
    diag = FOCAL * inv
    ux, uy = pts[0] * inv, pts[1] * inv
    row_x = [diag * (cam[e] - ux * cam[6 + e]) for e in range(3)]
    row_y = [diag * (cam[3 + e] - uy * cam[6 + e]) for e in range(3)]
    sxx, sxy, sxz, syy, syz, szz = sigma
    full = [[sxx, sxy, sxz], [sxy, syy, syz], [sxz, syz, szz]]
    half_x = [sum(full[i][e] * row_x[e] for e in range(3)) for i in range(3)]
    half_y = [sum(full[i][e] * row_y[e] for e in range(3)) for i in range(3)]
    cov_xx = sum(row_x[i] * half_x[i] for i in range(3)) + BLUR
    cov_xy = sum(row_y[i] * half_x[i] for i in range(3))
    cov_yy = sum(row_y[i] * half_y[i] for i in range(3)) + BLUR
    det = 1.0 / (cov_xx * cov_yy - cov_xy * cov_xy)
    return [
        FOCAL * ux + 0.5 * width_px,
        FOCAL * uy + 0.5 * height_px,
        cov_yy * det,
        -cov_xy * det,
        cov_xx * det,
    ]


def direction_basis(centers, cam):
    off = [centers[e] - cam[12 + e] for e in range(3)]
    inv = 1.0 / jnp.sqrt(sum(v * v for v in off))
    return harmonics(*[v * inv for v in off])


def small_row(small_ref, index, chunk):
    return small_ref[index, pl.ds(pl.multiple_of(chunk * 8, 8), 8), :]


def harm_slice(row, chunk):
    return pl.ds(((row // 8) * BLOCKS + chunk * 8) * 8 + row % 8, 8, stride=8)


def gather_blocks(tbl, index_hi, index_lo):
    acc = [jnp.zeros((8, LANES), F32) for _ in range(5)]
    for b in range(BLOCKS):
        hit = index_hi == b
        for i in range(5):
            got = jnp.take_along_axis(
                tbl[b * TBL + 8 * i : b * TBL + 8 * i + 8, :],
                index_lo,
                axis=1,
                mode="promise_in_bounds",
            )
            acc[i] = jnp.where(hit, got, acc[i])
    return acc


def slot_place(o):
    return (o // 16) * 8 + o % 8, (o // 8) % 2


def splat_out(width_px, height_px, cam_ref, small_ref, harm_ref, ids_ref, out_ref, tbl):
    def chunk_step(chunk, carry):
        centers = [small_row(small_ref, i, chunk) for i in range(3)]
        scales = [small_row(small_ref, 3 + i, chunk) for i in range(3)]
        rots = [small_row(small_ref, 6 + i, chunk) for i in range(4)]
        opacity = jax.nn.sigmoid(small_row(small_ref, 10, chunk))
        sigma = shape_of(scales, rots)
        base = chunk * (8 * TBL)
        for view in range(VIEWS):
            cam = [cam_ref[view, i] for i in range(15)]
            record = geometry(centers, sigma, cam, width_px, height_px) + [opacity]
            basis = direction_basis(centers, cam)
            for colour in range(3):
                total = sum(
                    harm_ref[harm_slice(colour * 16 + i, chunk), :] * basis[i]
                    for i in range(16)
                )
                record.append(jnp.maximum(total + 0.5, 0.0))
            for i in range(8):
                tbl[pl.ds(base + view * 8 + i, 8, stride=TBL), :] = record[i]
            tbl[pl.ds(base + 32 + view, 8, stride=TBL), :] = record[8]
        return carry

    lax.fori_loop(0, BLOCKS // 8, chunk_step, 0)

    def order_step(o, carry):
        index = jnp.broadcast_to(ids_ref[pl.ds(o, 1), :], (8, LANES))
        acc = gather_blocks(tbl, index >> 7, index & 127)
        owner, half = slot_place(o)
        for view in range(VIEWS):
            row = (view * 32 + owner) * MSG + half
            out_ref[pl.ds(row, 8, stride=2), :] = acc[view]
            out_ref[pl.ds(row + 16, 1), :] = acc[4][view : view + 1, :]
        return carry

    lax.fori_loop(0, BLOCKS, order_step, 0)


def top_f32(x):
    return x.astype(BF16).astype(F32)


def split(x):
    top = x.astype(BF16)
    return top, x - top.astype(F32)


def product(x, y):
    return jnp.dot(x, y, preferred_element_type=F32)


def summed(x, pattern):
    top, rest = split(x)
    return product(jnp.concatenate([top, rest.astype(BF16)], axis=1), pattern)


def tiles(
    perm_ref, recv_ref, list_ref, target_ref, out_ref, image_ref, loss_ref,
    tab, wide, target_t, image_t, rec, alpha, weight, ends, shades, prefix, res, behind,
    moments, grad, inverse, sums_ref,
):
    lane = lax.broadcasted_iota(I32, (8, LANES), 1)
    sub = lax.broadcasted_iota(I32, (8, LANES), 0)
    sub_f = sub.astype(F32)
    tall_lane = lax.broadcasted_iota(I32, (256, LANES), 1)
    from_lane = lax.broadcasted_iota(I32, (256, LANES), 0) % 128
    sums_ref[0] = (from_lane < tall_lane).astype(F32).astype(BF16)
    sums_ref[1] = jnp.ones((256, LANES), BF16)
    sums_ref[2] = (from_lane > tall_lane).astype(F32).astype(BF16)

    for half in range(2):
        for k in range(FIELDS):
            tab[k, half * 128 : half * 128 + 128, :] = recv_ref[
                pl.ds(k * 2 + half, 128, stride=MSG), :
            ].T
    wide[...] = jnp.zeros_like(wide)
    wide[0:48, :] = target_ref[...]
    for i in range(2):
        target_t[i * 128 : i * 128 + 128, :] = wide[:, i * 128 : i * 128 + 128].T
    image_t[...] = jnp.zeros_like(image_t)

    def take(x, index):
        return jnp.take_along_axis(x, index, axis=1, mode="promise_in_bounds")

    def tile_step(r, loss):
        place = perm_ref[r]
        ox = (16 * (place % TW)).astype(F32)
        oy = (16 * (place // TW)).astype(F32)
        row0 = (r // 8) * 128 + r % 8
        list_lo = list_ref[pl.ds(row0, 8, stride=8), :].astype(F32)
        list_hi = list_ref[pl.ds(row0 + 64, 8, stride=8), :].astype(F32)
        count = jnp.sum(
            (list_lo >= 0.0).astype(F32) + (list_hi >= 0.0).astype(F32)
        ).astype(I32)
        steps = (count + 127) // 128
        inverse[...] = jnp.zeros_like(inverse)
        tile_rows = pl.multiple_of(r * 16, 8)

        def load_step(j, carry):
            k = lane * steps + j
            block, low = k >> 7, k & 127
            entry = jnp.sum(
                jnp.where(block == sub, take(list_lo, low), 0.0)
                + jnp.where(block == sub + 8, take(list_hi, low), 0.0),
                axis=0,
                keepdims=True,
            ).astype(I32)
            entry = jnp.broadcast_to(entry, (8, LANES))
            source, slot = (entry >> 8) & 127, entry & 15
            hit0, hit1 = slot == sub, slot == sub + 8
            fields = []
            for f in range(FIELDS):
                got0 = take(tab[f, pl.ds(tile_rows, 8), :], source)
                got1 = take(tab[f, pl.ds(tile_rows + 8, 8), :], source)
                fields.append(
                    jnp.sum(
                        jnp.where(hit0, got0, jnp.where(hit1, got1, 0.0)),
                        axis=0,
                        keepdims=True,
                    )
                )
            listed = entry[0:1] >= 0
            mx, my = fields[0] - ox, fields[1] - oy
            opacity = jnp.where(listed, fields[5], 1.0)
            level = jnp.where(listed, jnp.log2(opacity), -1e30)
            for i, value in enumerate(
                [mx, my] + fields[2:5] + [opacity] + fields[6:9]
            ):
                rec[j, pl.ds(i, 1), :] = value
            qxx = (-0.5 * LOG2E) * fields[2]
            qxy = -LOG2E * fields[3]
            qyy = (-0.5 * LOG2E) * fields[4]
            parts = []
            for h in range(2):
                dx = (sub_f + 8.0 * h) - mx
                parts.append((qxy * dx, qxx * dx * dx + level))
            for y in range(16):
                dy = jnp.broadcast_to(float(y) - my, (8, LANES))
                turn = qyy * dy
                for h in range(2):
                    slope, level_h = parts[h]
                    alpha[j, y * 2 + h] = jnp.exp2((slope + turn) * dy + level_h)
            rows = lax.broadcasted_iota(I32, (128, LANES), 0)
            listed_b = entry >= 0
            one_hot = (rows == entry[0:1] >> 8).astype(F32)
            step_no = (j + 1).astype(F32)
            left = [
                jnp.where(hit0 & listed_b, step_no, 0.0),
                jnp.where(hit1 & listed_b, step_no, 0.0),
                jnp.where(hit0 & listed_b, lane.astype(F32), 0.0),
                jnp.where(hit1 & listed_b, lane.astype(F32), 0.0),
            ]
            inverse[...] += lax.dot_general(
                jnp.concatenate(left, axis=0).astype(BF16),
                one_hot.astype(BF16),
                (((1,), (1,)), ((), ())),
                preferred_element_type=F32,
            )
            return carry

        lax.fori_loop(0, steps, load_step, 0)

        for g in range(4):

            def front_step(j, carry):
                keep, col = list(carry[:8]), list(carry[8:])
                shade = [
                    jnp.broadcast_to(rec[j, pl.ds(6 + c, 1), :], (8, LANES)) for c in range(3)
                ]
                for i in range(8):
                    w = alpha[j, g * 8 + i] * keep[i]
                    weight[j, g * 8 + i] = w
                    keep[i] = keep[i] - w
                    for c in range(3):
                        col[i * 3 + c] = col[i * 3 + c] + shade[c] * w
                return tuple(keep + col)

            start = [jnp.ones((8, LANES), F32)] * 8 + [jnp.zeros((8, LANES), F32)] * 24
            done = lax.fori_loop(0, steps, front_step, tuple(start))
            for i in range(8):
                ends[g * 8 + i] = done[i]
                for c in range(3):
                    shades[c, g * 8 + i] = done[8 + i * 3 + c]

        def all_pixels(x):
            return x.reshape(256, LANES)

        local_end = all_pixels(ends[...])
        level_end = jnp.log2(local_end)
        top, rest_bits = split(level_end)
        low = (rest_bits - top_f32(rest_bits)).astype(BF16)
        front = jnp.exp2(
            product(jnp.concatenate([top, rest_bits.astype(BF16)], axis=1), sums_ref[0])
            + product(low, sums_ref[0, 0:128, :])
        )
        prefix[...] = front.reshape(32, 8, LANES)
        target = target_t[...]
        image = image_t[...]
        behind_all = jnp.zeros((256, LANES), F32)
        square = jnp.zeros((256, LANES), F32)
        for c in range(3):
            part = front * all_pixels(shades[c])
            mine = tall_lane == c * 16 + r
            diff = summed(part - jnp.where(mine, target, 0.0), sums_ref[1])
            res[c] = diff.reshape(32, 8, LANES)
            image = jnp.where(mine, diff + target, image)
            behind_all = behind_all + diff * part
            square = square + diff * diff
        image_t[...] = image
        behind[...] = (summed(behind_all, sums_ref[2]) / (front * local_end)).reshape(
            32, 8, LANES
        )
        loss = loss + jnp.sum(square.reshape(32, 8, LANES), axis=0)

        for g in range(4):

            def back_step(back_j, carry):
                back = list(carry)
                j = steps - 1 - back_j
                shade = [
                    jnp.broadcast_to(rec[j, pl.ds(6 + c, 1), :], (8, LANES)) for c in range(3)
                ]
                if g == 0:
                    sums = [jnp.zeros((8, LANES), F32)] * 9
                else:
                    sums = [moments[j, i] for i in range(9)]
                for i in range(8):
                    idx = g * 8 + i
                    h = i % 2
                    a = alpha[j, idx]
                    w = weight[j, idx] * prefix[idx]
                    diff = [res[c, idx] for c in range(3)]
                    u = shade[0] * diff[0] + shade[1] * diff[1] + shade[2] * diff[2] - back[i]
                    back[i] = back[i] + a * u
                    v = w * u
                    for c in range(3):
                        sums[6 + c] = sums[6 + c] + diff[c] * w
                    sums[3 * h] = sums[3 * h] + v
                    sums[3 * h + 1] = sums[3 * h + 1] + sums[3 * h]
                    sums[3 * h + 2] = sums[3 * h + 2] + sums[3 * h + 1]
                for i in range(9):
                    moments[j, i] = sums[i]
                return tuple(back)

            lax.fori_loop(0, steps, back_step, tuple(behind[g * 8 + i] for i in range(8)))

        def finish_step(j, carry):
            def total(x):
                return jnp.sum(x, axis=0, keepdims=True)

            s = [moments[j, i] for i in range(9)]
            x0, x1 = sub_f, sub_f + 8.0
            y1 = [16.0 * s[3 * h] - s[3 * h + 1] for h in range(2)]
            y2 = [256.0 * s[3 * h] - 33.0 * s[3 * h + 1] + 2.0 * s[3 * h + 2] for h in range(2)]
            m0 = total(s[0] + s[3])
            m_x = total(x0 * s[0] + x1 * s[3])
            m_xx = total(x0 * x0 * s[0] + x1 * x1 * s[3])
            m_y = total(y1[0] + y1[1])
            m_xy = total(x0 * y1[0] + x1 * y1[1])
            m_yy = total(y2[0] + y2[1])
            mx, my, xx, xy, yy, opacity = [rec[j, pl.ds(i, 1), :] for i in range(6)]
            g_x = m_x - mx * m0
            g_y = m_y - my * m0
            g_xx = m_xx - 2.0 * mx * m_x + mx * mx * m0
            g_xy = m_xy - mx * m_y - my * m_x + mx * my * m0
            g_yy = m_yy - 2.0 * my * m_y + my * my * m0
            out = [
                xx * g_x + xy * g_y,
                yy * g_y + xy * g_x,
                -0.5 * g_xx,
                -g_xy,
                -0.5 * g_yy,
                m0 / opacity,
            ] + [total(s[6 + c]) for c in range(3)]
            for i in range(FIELDS):
                grad[j, pl.ds(i, 1), :] = out[i]
            return carry

        lax.fori_loop(0, steps, finish_step, 0)

        step0 = inverse[0:8, :].astype(I32)
        step1 = inverse[8:16, :].astype(I32)
        lane0 = inverse[16:24, :].astype(I32)
        lane1 = inverse[24:32, :].astype(I32)

        def unlist_step(j, carry):
            acc = list(carry)
            hit0, hit1 = step0 == j + 1, step1 == j + 1
            for f in range(FIELDS):
                row = jnp.broadcast_to(grad[j, pl.ds(f, 1), :], (8, LANES))
                acc[2 * f] = jnp.where(hit0, take(row, lane0), acc[2 * f])
                acc[2 * f + 1] = jnp.where(hit1, take(row, lane1), acc[2 * f + 1])
            return tuple(acc)

        acc = lax.fori_loop(0, steps, unlist_step, (jnp.zeros((8, LANES), F32),) * 18)
        for f in range(FIELDS):
            tab[f, pl.ds(tile_rows, 8), :] = acc[2 * f]
            tab[f, pl.ds(tile_rows + 8, 8), :] = acc[2 * f + 1]
        return loss

    loss = lax.fori_loop(0, 16, tile_step, jnp.zeros((8, LANES), F32))
    loss_ref[...] = loss
    for half in range(2):
        for k in range(FIELDS):
            out_ref[pl.ds(k * 2 + half, 128, stride=MSG), :] = tab[
                k, half * 128 : half * 128 + 128, :
            ].T
    for i in range(2):
        wide[:, i * 128 : i * 128 + 128] = image_t[i * 128 : i * 128 + 128, :].T
    image_ref[...] = wide[0:48, :]


def splat_back(
    width_px, height_px, cam_ref, small_ref, harm_ref, ids_ref, ret_ref,
    gsmall_ref, gharm_ref, tbl, nat, inverse,
):
    lane = lax.broadcasted_iota(I32, (1, LANES), 1)
    rows64 = lax.broadcasted_iota(I32, (BLOCKS, LANES), 0)
    rows128 = lax.broadcasted_iota(I32, (LANES, LANES), 0)
    inverse[...] = jnp.zeros_like(inverse)

    def invert_step(o, carry):
        index = ids_ref[pl.ds(o, 1), :]
        hit = rows64 == index >> 7
        one_hot = (rows128 == index & 127).astype(F32).astype(BF16)
        left = jnp.concatenate(
            [
                jnp.where(hit, (o + 1).astype(F32), 0.0),
                jnp.where(hit, lane.astype(F32), 0.0),
            ],
            axis=0,
        )
        inverse[...] += lax.dot_general(
            left.astype(BF16),
            one_hot,
            (((1,), (1,)), ((), ())),
            preferred_element_type=F32,
        )
        owner, half = slot_place(o)
        base = o * TBL
        for view in range(VIEWS):
            row = (view * 32 + owner) * MSG + half
            tbl[pl.ds(base + view * 8, 8), :] = ret_ref[pl.ds(row, 8, stride=2), :]
            tbl[pl.ds(base + 32 + view, 1), :] = ret_ref[pl.ds(row + 16, 1), :]
        return carry

    lax.fori_loop(0, BLOCKS, invert_step, 0)

    def order_step(n, carry):
        block = jnp.broadcast_to(inverse[pl.ds(n, 1), :].astype(I32) - 1, (8, LANES))
        low = jnp.broadcast_to(inverse[pl.ds(BLOCKS + n, 1), :].astype(I32), (8, LANES))
        acc = gather_blocks(tbl, block, low)
        for i in range(5):
            nat[pl.ds(8 * i * BLOCKS + n, 8, stride=BLOCKS), :] = acc[i]
        return carry

    lax.fori_loop(0, BLOCKS, order_step, 0)

    def chunk_step(chunk, carry):
        centers = [small_row(small_ref, i, chunk) for i in range(3)]
        scales = [small_row(small_ref, 3 + i, chunk) for i in range(3)]
        rots = [small_row(small_ref, 6 + i, chunk) for i in range(4)]
        opacity = jax.nn.sigmoid(small_row(small_ref, 10, chunk))

        def given(view, i):
            row = view * 8 + i if i < 8 else 32 + view
            return nat[pl.ds(pl.multiple_of(row * BLOCKS + chunk * 8, 8), 8), :]

        sigma, shape_pull = jax.vjp(shape_of, scales, rots)
        d_centers = [jnp.zeros((8, LANES), F32)] * 3
        d_sigma = [jnp.zeros((8, LANES), F32)] * 6
        d_opacity = jnp.zeros((8, LANES), F32)
        for view in range(VIEWS):
            cam = [cam_ref[view, i] for i in range(15)]
            _, geo_pull = jax.vjp(
                lambda c, s: geometry(c, s, cam, width_px, height_px), centers, sigma
            )
            d_c, d_s = geo_pull([given(view, i) for i in range(5)])
            basis, dir_pull = jax.vjp(lambda c: direction_basis(c, cam), centers)
            d_opacity = d_opacity + given(view, 5)
            d_basis = [jnp.zeros((8, LANES), F32)] * 16
            for colour in range(3):
                rows = [harm_slice(colour * 16 + i, chunk) for i in range(16)]
                coeffs = [harm_ref[row, :] for row in rows]
                total = sum(coeffs[i] * basis[i] for i in range(16)) + 0.5
                slope = jnp.where(total > 0.0, 1.0, jnp.where(total == 0.0, 0.5, 0.0))
                d_total = given(view, 6 + colour) * slope
                for i in range(16):
                    d_basis[i] = d_basis[i] + d_total * coeffs[i]
                    term = d_total * basis[i]
                    if view == 0:
                        gharm_ref[rows[i], :] = term
                    else:
                        gharm_ref[rows[i], :] = gharm_ref[rows[i], :] + term
            (d_dir,) = dir_pull(d_basis)
            d_centers = [d_centers[e] + d_c[e] + d_dir[e] for e in range(3)]
            d_sigma = [d_sigma[e] + d_s[e] for e in range(6)]
        d_scales, d_rots = shape_pull(d_sigma)
        values = (
            list(d_centers)
            + list(d_scales)
            + list(d_rots)
            + [d_opacity * opacity * (1.0 - opacity)]
        )
        for i in range(11):
            gsmall_ref[i, pl.ds(pl.multiple_of(chunk * 8, 8), 8), :] = values[i]
        return carry

    lax.fori_loop(0, BLOCKS // 8, chunk_step, 0)


def tile_order(x):
    rows, width = x.shape
    split = x.reshape(rows // 8, 8, width // LANES, LANES)
    return split.transpose(0, 2, 1, 3).reshape(rows * width // LANES, LANES)


def from_tile_order(x, rows):
    width = x.shape[0] * LANES // rows
    split = x.reshape(rows // 8, width // LANES, 8, LANES)
    return split.transpose(0, 2, 1, 3).reshape(rows, width)


def params(mib):
    return pltpu.CompilerParams(vmem_limit_bytes=mib * 1024 * 1024)


def shape(*dims):
    return jax.ShapeDtypeStruct(dims, F32)


VM = functools.partial(pl.BlockSpec, memory_space=pltpu.VMEM)
SM = functools.partial(pl.BlockSpec, memory_space=pltpu.SMEM)


def exchange(message):
    blocks = message.reshape(128, MSG, LANES)
    return lax.all_to_all(
        blocks, ("view", "pix"), split_axis=0, concat_axis=0, tiled=True
    ).reshape(128 * MSG, LANES)


def local(
    centers, log_scales, rotations, logits, harmonic_coeffs,
    cameras, send_ids, tile_lists, tile_perm, targets,
):
    width_px = 16 * TW
    height_px = 16 * (512 // TW)
    cam = camera_numbers(cameras)
    small = jnp.concatenate(
        [centers, log_scales, rotations, logits[None]], axis=0
    ).reshape(11, BLOCKS, LANES)
    harm = tile_order(harmonic_coeffs)
    ids = tile_order(send_ids[0])
    sending = pl.pallas_call(
        functools.partial(splat_out, width_px, height_px),
        out_shape=shape(128 * MSG, LANES),
        in_specs=[SM(), VM(), VM(), VM()],
        out_specs=VM(),
        scratch_shapes=[pltpu.VMEM((BLOCKS * TBL, LANES), F32)],
        compiler_params=params(32),
        name="splat_out",
    )(cam, small, harm, ids)
    received = exchange(sending)
    vreg = (8, LANES)
    returning, image, loss = pl.pallas_call(
        tiles,
        out_shape=(shape(128 * MSG, LANES), shape(48, 256), shape(8, LANES)),
        in_specs=[SM(), VM(), VM(), VM()],
        out_specs=(VM(), VM(), VM()),
        scratch_shapes=[
            pltpu.VMEM((FIELDS, 256, LANES), F32),
            pltpu.VMEM((LANES, 256), F32),
            pltpu.VMEM((256, LANES), F32),
            pltpu.VMEM((256, LANES), F32),
            pltpu.VMEM((16, 16, LANES), F32),
            pltpu.VMEM((16, 32) + vreg, F32),
            pltpu.VMEM((16, 32) + vreg, F32),
            pltpu.VMEM((32,) + vreg, F32),
            pltpu.VMEM((3, 32) + vreg, F32),
            pltpu.VMEM((32,) + vreg, F32),
            pltpu.VMEM((3, 32) + vreg, F32),
            pltpu.VMEM((32,) + vreg, F32),
            pltpu.VMEM((16, 9) + vreg, F32),
            pltpu.VMEM((16, 16, LANES), F32),
            pltpu.VMEM((32, LANES), F32),
            pltpu.VMEM((3, 256, LANES), BF16),
        ],
        compiler_params=params(48),
        name="tiles",
    )(
        tile_perm,
        received,
        tile_order(tile_lists),
        targets[0].transpose(1, 0, 2).reshape(48, 256),
    )
    returned = exchange(returning)
    total_loss = lax.psum(0.5 * jnp.sum(loss[:, 0]), ("view", "pix"))
    gsmall, gharm = pl.pallas_call(
        functools.partial(splat_back, width_px, height_px),
        out_shape=(shape(11, BLOCKS, LANES), shape(48 * BLOCKS, LANES)),
        in_specs=[SM(), VM(), VM(), VM(), VM()],
        out_specs=(VM(), VM()),
        scratch_shapes=[
            pltpu.VMEM((BLOCKS * TBL, LANES), F32),
            pltpu.VMEM((BLOCKS * TBL, LANES), F32),
            pltpu.VMEM((2 * BLOCKS, LANES), F32),
        ],
        compiler_params=params(32),
        name="splat_back",
    )(cam, small, harm, ids, returned)
    flat = gsmall.reshape(11, BLOCKS * LANES)
    rendered = image.reshape(3, 16, 256).transpose(1, 0, 2)[None]
    return (
        rendered,
        total_loss,
        flat[0:3],
        flat[3:6],
        flat[6:10],
        flat[10],
        from_tile_order(gharm, 48),
    )


def solution(mesh):
    both = ("view", "pix")
    return jax.shard_map(
        local,
        mesh=mesh,
        in_specs=(
            P(None, both),
            P(None, both),
            P(None, both),
            P(both),
            P(None, both),
            P(),
            P(both, None, None),
            P("pix", None),
            P("pix"),
            P("view", "pix", None, None),
        ),
        out_specs=(
            P("view", "pix", None, None),
            P(),
            P(None, both),
            P(None, both),
            P(None, both),
            P(both),
            P(None, both),
        ),
        check_vma=False,
    )
```

```python
import functools

import jax
import jax.numpy as jnp
from jax import lax
from jax.experimental import pallas as pl
from jax.experimental.pallas import tpu as pltpu
from jax.sharding import PartitionSpec as P

TW = 16
FOCAL = 1100.0
BLUR = 0.3
SH_ZERO = 0.28209479177387814
SH_ONE = 0.4886025119029199
SH_TWO = (
    1.0925484305920792,
    -1.0925484305920792,
    0.31539156525252005,
    -1.0925484305920792,
    0.5462742152960396,
)
SH_THREE = (
    -0.5900435899266435,
    2.890611442640554,
    -0.4570457994644658,
    0.3731763325901154,
    -0.4570457994644658,
    1.445305721320277,
    -0.5900435899266435,
)
LOG2E = 1.4426950408889634
LANES = 128
VIEWS = 4
FIELDS = 9
MSG = 24
LOSS_ROW = 18
TBL = 40
BLOCKS = 64
F32 = jnp.float32
I32 = jnp.int32
BF16 = jnp.bfloat16


def camera_numbers(cameras):
    cos, sin = jnp.cos(cameras[:, :3]), jnp.sin(cameras[:, :3])
    ca, cb, cc = cos[:, 0], cos[:, 1], cos[:, 2]
    sa, sb, sc = sin[:, 0], sin[:, 1], sin[:, 2]
    turn = [
        [cc * cb, cc * sb * sa - sc * ca, cc * sb * ca + sc * sa],
        [sc * cb, sc * sb * sa + cc * ca, sc * sb * ca - cc * sa],
        [-sb, cb * sa, cb * ca],
    ]
    shift = [cameras[:, 3], cameras[:, 4], cameras[:, 5]]
    anchor = [-sum(turn[i][e] * shift[i] for i in range(3)) for e in range(3)]
    return jnp.stack(turn[0] + turn[1] + turn[2] + shift + anchor + [shift[0]], axis=1)


def harmonics(x, y, z):
    xx, yy, zz = x * x, y * y, z * z
    return [
        SH_ZERO * jnp.ones_like(x),
        -SH_ONE * y,
        SH_ONE * z,
        -SH_ONE * x,
        SH_TWO[0] * x * y,
        SH_TWO[1] * y * z,
        SH_TWO[2] * (2.0 * zz - xx - yy),
        SH_TWO[3] * x * z,
        SH_TWO[4] * (xx - yy),
        SH_THREE[0] * y * (3.0 * xx - yy),
        SH_THREE[1] * x * y * z,
        SH_THREE[2] * y * (4.0 * zz - xx - yy),
        SH_THREE[3] * z * (2.0 * zz - 3.0 * xx - 3.0 * yy),
        SH_THREE[4] * x * (4.0 * zz - xx - yy),
        SH_THREE[5] * z * (xx - yy),
        SH_THREE[6] * x * (xx - 3.0 * yy),
    ]


def shape_of(scales, rots):
    inv = 1.0 / jnp.sqrt(sum(q * q for q in rots))
    s, x, y, z = [q * inv for q in rots]
    turn = [
        [1.0 - 2.0 * (y * y + z * z), 2.0 * (x * y - s * z), 2.0 * (x * z + s * y)],
        [2.0 * (x * y + s * z), 1.0 - 2.0 * (x * x + z * z), 2.0 * (y * z - s * x)],
        [2.0 * (x * z - s * y), 2.0 * (y * z + s * x), 1.0 - 2.0 * (x * x + y * y)],
    ]
    spread = [jnp.exp(v) for v in scales]
    m = [[turn[i][e] * spread[e] for e in range(3)] for i in range(3)]
    pairs = ((0, 0), (0, 1), (0, 2), (1, 1), (1, 2), (2, 2))
    return [sum(m[i][e] * m[k][e] for e in range(3)) for i, k in pairs]


def geometry(centers, sigma, cam, width_px, height_px):
    pts = [
        sum(cam[3 * i + e] * centers[e] for e in range(3)) + cam[9 + i] for i in range(3)
    ]
    inv = 1.0 / pts[2]
    diag = FOCAL * inv
    ux, uy = pts[0] * inv, pts[1] * inv
    row_x = [diag * (cam[e] - ux * cam[6 + e]) for e in range(3)]
    row_y = [diag * (cam[3 + e] - uy * cam[6 + e]) for e in range(3)]
    sxx, sxy, sxz, syy, syz, szz = sigma
    full = [[sxx, sxy, sxz], [sxy, syy, syz], [sxz, syz, szz]]
    half_x = [sum(full[i][e] * row_x[e] for e in range(3)) for i in range(3)]
    half_y = [sum(full[i][e] * row_y[e] for e in range(3)) for i in range(3)]
    cov_xx = sum(row_x[i] * half_x[i] for i in range(3)) + BLUR
    cov_xy = sum(row_y[i] * half_x[i] for i in range(3))
    cov_yy = sum(row_y[i] * half_y[i] for i in range(3)) + BLUR
    det = 1.0 / (cov_xx * cov_yy - cov_xy * cov_xy)
    return [
        FOCAL * ux + 0.5 * width_px,
        FOCAL * uy + 0.5 * height_px,
        cov_yy * det,
        -cov_xy * det,
        cov_xx * det,
    ]


def direction_basis(centers, cam):
    off = [centers[e] - cam[12 + e] for e in range(3)]
    inv = 1.0 / jnp.sqrt(sum(v * v for v in off))
    return harmonics(*[v * inv for v in off])


def small_row(small_ref, index, chunk):
    return small_ref[index, pl.ds(pl.multiple_of(chunk * 8, 8), 8), :]


def harm_slice(row, chunk):
    return pl.ds(((row // 8) * BLOCKS + chunk * 8) * 8 + row % 8, 8, stride=8)


def slot_place(o):
    return (o // 16) * 8 + o % 8, (o // 8) % 2


def splat_out(width_px, height_px, cam_ref, small_ref, harm_ref, ids_ref, out_ref, tbl, by_row, stage):
    def chunk_step(chunk, carry):
        centers = [small_row(small_ref, i, chunk) for i in range(3)]
        scales = [small_row(small_ref, 3 + i, chunk) for i in range(3)]
        rots = [small_row(small_ref, 6 + i, chunk) for i in range(4)]
        opacity = jax.nn.sigmoid(small_row(small_ref, 10, chunk))
        sigma = shape_of(scales, rots)
        base = chunk * (8 * TBL)
        for view in range(VIEWS):
            cam = [cam_ref[view, i] for i in range(15)]
            record = geometry(centers, sigma, cam, width_px, height_px) + [opacity]
            basis = direction_basis(centers, cam)
            for colour in range(3):
                total = sum(
                    harm_ref[harm_slice(colour * 16 + i, chunk), :] * basis[i]
                    for i in range(16)
                )
                record.append(jnp.maximum(total + 0.5, 0.0))
            for i in range(8):
                tbl[pl.ds(base + view * 8 + i, 8, stride=TBL), :] = record[i]
            tbl[pl.ds(base + 32 + view, 8, stride=TBL), :] = record[8]
        return carry

    lax.fori_loop(0, BLOCKS // 8, chunk_step, 0)

    def turn_step(group, carry):
        for u in range(4):
            b = group * 4 + u
            block = tbl[pl.ds(pl.multiple_of(b * TBL, 8), TBL), :]
            by_row[pl.ds(pl.multiple_of(b * LANES, 8), LANES), 0:TBL] = block.T
        return carry

    lax.fori_loop(0, BLOCKS // 4, turn_step, 0)
    by_row[BLOCKS * LANES : BLOCKS * LANES + 8, :] = jnp.zeros((8, LANES), F32)

    def order_step(group, carry):
        for u in range(4):
            o = group * 4 + u
            for c in range(LANES):
                stage[u, c : c + 1, :] = by_row[pl.ds(ids_ref[o, c], 1), :]
        for u in range(4):
            acc = stage[u, :, 0:TBL].T
            owner, half = slot_place(group * 4 + u)
            for view in range(VIEWS):
                row = (view * 32 + owner) * MSG + half
                out_ref[pl.ds(row, 8, stride=2), :] = acc[view * 8 : view * 8 + 8, :]
                out_ref[pl.ds(row + 16, 1), :] = acc[32 + view : 33 + view, :]
        return carry

    lax.fori_loop(0, BLOCKS // 4, order_step, 0)


def top_f32(x):
    return x.astype(BF16).astype(F32)


def split(x):
    top = x.astype(BF16)
    return top, x - top.astype(F32)


def product(x, y):
    return jnp.dot(x, y, preferred_element_type=F32)


def summed(x, pattern):
    top, rest = split(x)
    return product(jnp.concatenate([top, rest.astype(BF16)], axis=1), pattern)


def tiles(
    perm_ref, recv_ref, list_ref, target_ref, out_ref, image_ref,
    tab, wide, target_t, image_t, rec, lines, alpha, weight, ends, shades, prefix, res, behind,
    moments, grad, inverse, sums_ref,
):
    lane = lax.broadcasted_iota(I32, (8, LANES), 1)
    sub = lax.broadcasted_iota(I32, (8, LANES), 0)
    sub_f = sub.astype(F32)
    lane_f = lane.astype(F32)
    rows = lax.broadcasted_iota(I32, (LANES, LANES), 0)
    wide_lane = lax.broadcasted_iota(I32, (LANES, LANES), 1)
    tall_lane = lax.broadcasted_iota(I32, (256, LANES), 1)
    from_lane = lax.broadcasted_iota(I32, (256, LANES), 0) % 128
    sums_ref[0] = (from_lane < tall_lane).astype(F32).astype(BF16)
    sums_ref[1] = jnp.ones((256, LANES), BF16)
    sums_ref[2] = (from_lane > tall_lane).astype(F32).astype(BF16)

    for half in range(2):
        for k in range(FIELDS):
            tab[k, half * 128 : half * 128 + 128, :] = recv_ref[
                pl.ds(k * 2 + half, 128, stride=MSG), :
            ].T
    wide[...] = jnp.zeros_like(wide)
    wide[0:48, :] = target_ref[...]
    for i in range(2):
        target_t[i * 128 : i * 128 + 128, :] = wide[:, i * 128 : i * 128 + 128].T
    image_t[...] = jnp.zeros_like(image_t)

    def take(x, index):
        return jnp.take_along_axis(x, index, axis=1, mode="promise_in_bounds")

    def tile_step(r, carry):
        place = perm_ref[r]
        ox = (16 * (place % TW)).astype(F32)
        oy = (16 * (place // TW)).astype(F32)
        row0 = (r // 8) * 128 + r % 8
        list_lo = list_ref[pl.ds(row0, 8, stride=8), :].astype(F32)
        list_hi = list_ref[pl.ds(row0 + 64, 8, stride=8), :].astype(F32)
        count = jnp.sum(
            (list_lo >= 0.0).astype(F32) + (list_hi >= 0.0).astype(F32)
        ).astype(I32)
        steps = (count + 127) // 128
        pairs = (steps + 1) // 2
        quads = (steps + 3) // 4
        inverse[...] = jnp.zeros_like(inverse)
        tile_rows = pl.multiple_of(r * 16, 8)

        def load_step(group, carry):
            many = [group * 4 + u for u in range(4)]
            entries, masks, records = [], [], []
            for j in many:
                k = lane * steps + j
                block, low = k >> 7, k & 127
                found = jnp.sum(
                    jnp.where(block == sub, take(list_lo, low), 0.0)
                    + jnp.where(block == sub + 8, take(list_hi, low), 0.0),
                    axis=0,
                    keepdims=True,
                ).astype(I32)
                entries.append(jnp.broadcast_to(jnp.where(j < steps, found, -1), (8, LANES)))
            for entry in entries:
                masks.append((entry & 15 == sub, entry & 15 == sub + 8))
                records.append([])
            for f in range(FIELDS):
                half0 = tab[f, pl.ds(tile_rows, 8), :]
                half1 = tab[f, pl.ds(tile_rows + 8, 8), :]
                for entry, (hit0, hit1), fields in zip(entries, masks, records):
                    source = (entry >> 8) & 127
                    got = jnp.where(
                        hit0, take(half0, source), jnp.where(hit1, take(half1, source), 0.0)
                    )
                    fields.append(jnp.sum(got, axis=0, keepdims=True))
            lefts, rights = [], []
            for j, entry, (hit0, hit1) in zip(many, entries, masks):
                listed = entry >= 0
                step_no = (j + 1).astype(F32)
                spots = [jnp.where(listed, step_no, 0.0), jnp.where(listed, lane_f, 0.0)]
                left = [jnp.where(hit, spot, 0.0) for spot in spots for hit in (hit0, hit1)]
                lefts.append(jnp.concatenate(left, axis=0).astype(BF16))
                rights.append((rows == entry[0:1] >> 8).astype(F32).astype(BF16))
            inverse[...] += lax.dot_general(
                jnp.concatenate(lefts, axis=1),
                jnp.concatenate(rights, axis=1),
                (((1,), (1,)), ((), ())),
                preferred_element_type=F32,
            )
            for j, entry, fields in zip(many, entries, records):
                listed = entry[0:1] >= 0
                mx, my = fields[0] - ox, fields[1] - oy
                opacity = jnp.where(listed, fields[5], 1.0)
                level = jnp.where(listed, jnp.log2(opacity), -1e30)
                qyy = (-0.5 * LOG2E) * fields[4]
                values = [mx, my] + fields[2:5] + [opacity] + fields[6:9] + [qyy]
                for i, value in enumerate(values):
                    rec[j, pl.ds(i, 1), :] = value
                qxx = (-0.5 * LOG2E) * fields[2]
                qxy = -LOG2E * fields[3]
                for h in range(2):
                    dx = (sub_f + 8.0 * h) - mx
                    lines[j, 2 * h] = qxy * dx
                    lines[j, 2 * h + 1] = qxx * dx * dx + level
            return carry

        lax.fori_loop(0, quads, load_step, 0)

        def spread(j, i):
            return jnp.broadcast_to(rec[j, pl.ds(i, 1), :], (8, LANES))

        for g in range(4):

            def front_step(pair, carry):
                keep, col = list(carry[:8]), list(carry[8:])
                for j in (pair * 2, pair * 2 + 1):
                    shade = [spread(j, 6 + c) for c in range(3)]
                    my, qyy = spread(j, 1), spread(j, 9)
                    slope = [lines[j, 0], lines[j, 2]]
                    level = [lines[j, 1], lines[j, 3]]
                    for i in range(8):
                        if i % 2 == 0:
                            dy = float(g * 4 + i // 2) - my
                            turn = qyy * dy
                        a = jnp.exp2((slope[i % 2] + turn) * dy + level[i % 2])
                        alpha[j, g * 8 + i] = a
                        w = a * keep[i]
                        weight[j, g * 8 + i] = w
                        keep[i] = keep[i] - w
                        for c in range(3):
                            col[i * 3 + c] = col[i * 3 + c] + shade[c] * w
                return tuple(keep + col)

            start = [jnp.ones((8, LANES), F32)] * 8 + [jnp.zeros((8, LANES), F32)] * 24
            done = lax.fori_loop(0, pairs, front_step, tuple(start))
            for i in range(8):
                ends[g * 8 + i] = done[i]
                for c in range(3):
                    shades[c, g * 8 + i] = done[8 + i * 3 + c]

        for half in range(2):
            part_of = slice(half * 16, half * 16 + 16)
            pixels = slice(half * 128, half * 128 + 128)
            local_end = ends[part_of].reshape(128, LANES)
            top, rest = split(jnp.log2(local_end))
            low = (rest - top_f32(rest)).astype(BF16)
            front = jnp.exp2(
                product(jnp.concatenate([top, rest.astype(BF16)], axis=1), sums_ref[0])
                + product(low, sums_ref[0, 0:128, :])
            )
            prefix[part_of] = front.reshape(16, 8, LANES)
            image = image_t[pixels, :]
            behind_all = jnp.zeros((128, LANES), F32)
            for c in range(3):
                part = front * shades[c, part_of].reshape(128, LANES)
                mine = wide_lane == c * 16 + r
                target = target_t[pixels, :]
                diff = summed(part - jnp.where(mine, target, 0.0), sums_ref[1])
                res[c, part_of] = diff.reshape(16, 8, LANES)
                image = jnp.where(mine, diff + target, image)
                behind_all = behind_all + diff * part
            image_t[pixels, :] = image
            behind[part_of] = (summed(behind_all, sums_ref[2]) / (front * local_end)).reshape(
                16, 8, LANES
            )

        for g in range(4):

            def back_step(back_pair, carry):
                pair = pairs - 1 - back_pair
                return one_back(pair * 2, one_back(pair * 2 + 1, carry))

            def one_back(j, carry):
                back = list(carry)
                shade = [spread(j, 6 + c) for c in range(3)]
                if g == 0:
                    sums = [jnp.zeros((8, LANES), F32)] * 9
                else:
                    sums = [moments[j, i] for i in range(9)]
                for i in range(8):
                    idx = g * 8 + i
                    h = i % 2
                    a = alpha[j, idx]
                    w = weight[j, idx] * prefix[idx]
                    diff = [res[c, idx] for c in range(3)]
                    u = shade[0] * diff[0] + shade[1] * diff[1] + shade[2] * diff[2] - back[i]
                    back[i] = back[i] + a * u
                    v = w * u
                    for c in range(3):
                        sums[6 + c] = sums[6 + c] + diff[c] * w
                    sums[3 * h] = sums[3 * h] + v
                    sums[3 * h + 1] = sums[3 * h + 1] + sums[3 * h]
                    sums[3 * h + 2] = sums[3 * h + 2] + sums[3 * h + 1]
                for i in range(9):
                    moments[j, i] = sums[i]
                return tuple(back)

            lax.fori_loop(0, pairs, back_step, tuple(behind[g * 8 + i] for i in range(8)))

        def finish_step(group, carry):
            for u in range(4):
                finish(group * 4 + u)
            return carry

        def finish(j):
            def total(x):
                return jnp.sum(x, axis=0, keepdims=True)

            s = [moments[j, i] for i in range(9)]
            x0, x1 = sub_f, sub_f + 8.0
            y1 = [16.0 * s[3 * h] - s[3 * h + 1] for h in range(2)]
            y2 = [256.0 * s[3 * h] - 33.0 * s[3 * h + 1] + 2.0 * s[3 * h + 2] for h in range(2)]
            m0 = total(s[0] + s[3])
            m_x = total(x0 * s[0] + x1 * s[3])
            m_xx = total(x0 * x0 * s[0] + x1 * x1 * s[3])
            m_y = total(y1[0] + y1[1])
            m_xy = total(x0 * y1[0] + x1 * y1[1])
            m_yy = total(y2[0] + y2[1])
            mx, my, xx, xy, yy, opacity = [rec[j, pl.ds(i, 1), :] for i in range(6)]
            g_x = m_x - mx * m0
            g_y = m_y - my * m0
            g_xx = m_xx - 2.0 * mx * m_x + mx * mx * m0
            g_xy = m_xy - mx * m_y - my * m_x + mx * my * m0
            g_yy = m_yy - 2.0 * my * m_y + my * my * m0
            out = [
                xx * g_x + xy * g_y,
                yy * g_y + xy * g_x,
                -0.5 * g_xx,
                -g_xy,
                -0.5 * g_yy,
                m0 / opacity,
            ] + [total(s[6 + c]) for c in range(3)]
            for i in range(FIELDS):
                grad[j, pl.ds(i, 1), :] = out[i]

        lax.fori_loop(0, quads, finish_step, 0)

        step0 = inverse[0:8, :].astype(I32)
        step1 = inverse[8:16, :].astype(I32)
        lane0 = inverse[16:24, :].astype(I32)
        lane1 = inverse[24:32, :].astype(I32)

        def unlist_step(group, carry):
            acc = list(carry)
            for j in [group * 4 + u for u in range(4)]:
                hit0, hit1 = step0 == j + 1, step1 == j + 1
                for f in range(FIELDS):
                    row = jnp.broadcast_to(grad[j, pl.ds(f, 1), :], (8, LANES))
                    acc[2 * f] = jnp.where(hit0, take(row, lane0), acc[2 * f])
                    acc[2 * f + 1] = jnp.where(hit1, take(row, lane1), acc[2 * f + 1])
            return tuple(acc)

        acc = lax.fori_loop(0, quads, unlist_step, (jnp.zeros((8, LANES), F32),) * 18)
        for f in range(FIELDS):
            tab[f, pl.ds(tile_rows, 8), :] = acc[2 * f]
            tab[f, pl.ds(tile_rows + 8, 8), :] = acc[2 * f + 1]
        return carry

    lax.fori_loop(0, 16, tile_step, 0)
    errors = image_t[...] - target_t[...]
    total = jnp.sum(errors * errors, axis=0, keepdims=True)
    out_ref[pl.ds(LOSS_ROW, 128, stride=MSG), :] = jnp.broadcast_to(total, (128, LANES))
    for half in range(2):
        for k in range(FIELDS):
            out_ref[pl.ds(k * 2 + half, 128, stride=MSG), :] = tab[
                k, half * 128 : half * 128 + 128, :
            ].T
    for i in range(2):
        wide[:, i * 128 : i * 128 + 128] = image_t[i * 128 : i * 128 + 128, :].T
    image_ref[...] = wide[0:48, :]


def splat_back(
    width_px, height_px, cam_ref, small_ref, harm_ref, ids_ref, ret_ref,
    gsmall_ref, gharm_ref, loss_ref, nat, by_row, stage,
):
    losses = jnp.sum(ret_ref[pl.ds(LOSS_ROW, 128, stride=MSG), :], axis=0, keepdims=True)
    loss_ref[0, 0] = 0.5 * jnp.sum(losses)

    def clear_step(b, carry):
        by_row[pl.ds(pl.multiple_of(b * LANES, 8), LANES), :] = jnp.zeros((LANES, LANES), F32)
        return carry

    lax.fori_loop(0, BLOCKS, clear_step, 0)

    def order_step(group, carry):
        for u in range(4):
            owner, half = slot_place(group * 4 + u)
            rows = [(view * 32 + owner) * MSG + half for view in range(VIEWS)]
            parts = [ret_ref[pl.ds(row, 8, stride=2), :] for row in rows]
            parts += [ret_ref[pl.ds(row + 16, 1), :] for row in rows]
            parts.append(jnp.zeros((4, LANES), F32))
            stage[u, :, 0:TBL] = jnp.concatenate(parts, axis=0).T
        for u in range(4):
            for c in range(LANES):
                by_row[pl.ds(ids_ref[group * 4 + u, c], 1), :] = stage[u, c : c + 1, :]
        return carry

    lax.fori_loop(0, BLOCKS // 4, order_step, 0)

    def turn_step(group, carry):
        for u in range(4):
            n = group * 4 + u
            block = by_row[pl.ds(pl.multiple_of(n * LANES, 8), LANES), 0:TBL].T
            for i in range(5):
                nat[pl.ds(8 * i * BLOCKS + n, 8, stride=BLOCKS), :] = block[8 * i : 8 * i + 8, :]
        return carry

    lax.fori_loop(0, BLOCKS // 4, turn_step, 0)

    def chunk_step(chunk, carry):
        centers = [small_row(small_ref, i, chunk) for i in range(3)]
        scales = [small_row(small_ref, 3 + i, chunk) for i in range(3)]
        rots = [small_row(small_ref, 6 + i, chunk) for i in range(4)]
        opacity = jax.nn.sigmoid(small_row(small_ref, 10, chunk))

        def given(view, i):
            row = view * 8 + i if i < 8 else 32 + view
            return nat[pl.ds(pl.multiple_of(row * BLOCKS + chunk * 8, 8), 8), :]

        sigma, shape_pull = jax.vjp(shape_of, scales, rots)
        d_centers = [jnp.zeros((8, LANES), F32)] * 3
        d_sigma = [jnp.zeros((8, LANES), F32)] * 6
        d_opacity = jnp.zeros((8, LANES), F32)
        for view in range(VIEWS):
            cam = [cam_ref[view, i] for i in range(15)]
            _, geo_pull = jax.vjp(
                lambda c, s: geometry(c, s, cam, width_px, height_px), centers, sigma
            )
            d_c, d_s = geo_pull([given(view, i) for i in range(5)])
            basis, dir_pull = jax.vjp(lambda c: direction_basis(c, cam), centers)
            d_opacity = d_opacity + given(view, 5)
            d_basis = [jnp.zeros((8, LANES), F32)] * 16
            for colour in range(3):
                rows = [harm_slice(colour * 16 + i, chunk) for i in range(16)]
                coeffs = [harm_ref[row, :] for row in rows]
                total = sum(coeffs[i] * basis[i] for i in range(16)) + 0.5
                slope = jnp.where(total > 0.0, 1.0, jnp.where(total == 0.0, 0.5, 0.0))
                d_total = given(view, 6 + colour) * slope
                for i in range(16):
                    d_basis[i] = d_basis[i] + d_total * coeffs[i]
                    term = d_total * basis[i]
                    if view == 0:
                        gharm_ref[rows[i], :] = term
                    else:
                        gharm_ref[rows[i], :] = gharm_ref[rows[i], :] + term
            (d_dir,) = dir_pull(d_basis)
            d_centers = [d_centers[e] + d_c[e] + d_dir[e] for e in range(3)]
            d_sigma = [d_sigma[e] + d_s[e] for e in range(6)]
        d_scales, d_rots = shape_pull(d_sigma)
        values = (
            list(d_centers)
            + list(d_scales)
            + list(d_rots)
            + [d_opacity * opacity * (1.0 - opacity)]
        )
        for i in range(11):
            gsmall_ref[i, pl.ds(pl.multiple_of(chunk * 8, 8), 8), :] = values[i]
        return carry

    lax.fori_loop(0, BLOCKS // 8, chunk_step, 0)


def tile_order(x):
    rows, width = x.shape
    split = x.reshape(rows // 8, 8, width // LANES, LANES)
    return split.transpose(0, 2, 1, 3).reshape(rows * width // LANES, LANES)


def from_tile_order(x, rows):
    width = x.shape[0] * LANES // rows
    split = x.reshape(rows // 8, width // LANES, 8, LANES)
    return split.transpose(0, 2, 1, 3).reshape(rows, width)


def params(mib):
    return pltpu.CompilerParams(vmem_limit_bytes=mib * 1024 * 1024)


def shape(*dims):
    return jax.ShapeDtypeStruct(dims, F32)


VM = functools.partial(pl.BlockSpec, memory_space=pltpu.VMEM)
SM = functools.partial(pl.BlockSpec, memory_space=pltpu.SMEM)


def exchange(message):
    blocks = message.reshape(128, MSG, LANES)
    return lax.all_to_all(
        blocks, ("view", "pix"), split_axis=0, concat_axis=0, tiled=True
    ).reshape(128 * MSG, LANES)


def local(
    centers, log_scales, rotations, logits, harmonic_coeffs,
    cameras, send_ids, tile_lists, tile_perm, targets,
):
    width_px = 16 * TW
    height_px = 16 * (512 // TW)
    cam = camera_numbers(cameras)
    small = jnp.concatenate(
        [centers, log_scales, rotations, logits[None]], axis=0
    ).reshape(11, BLOCKS, LANES)
    harm = tile_order(harmonic_coeffs)
    ids = tile_order(send_ids[0])
    ids = jnp.where(ids >= 0, ids, BLOCKS * LANES)
    sending = pl.pallas_call(
        functools.partial(splat_out, width_px, height_px),
        out_shape=shape(128 * MSG, LANES),
        in_specs=[SM(), VM(), VM(), SM()],
        out_specs=VM(),
        scratch_shapes=[
            pltpu.VMEM((BLOCKS * TBL, LANES), F32),
            pltpu.VMEM((BLOCKS * LANES + 8, LANES), F32),
            pltpu.VMEM((4, LANES, LANES), F32),
        ],
        compiler_params=params(32),
        name="splat_out",
    )(cam, small, harm, ids)
    received = exchange(sending)
    vreg = (8, LANES)
    returning, image = pl.pallas_call(
        tiles,
        out_shape=(shape(128 * MSG, LANES), shape(48, 256)),
        in_specs=[SM(), VM(), VM(), VM()],
        out_specs=(VM(), VM()),
        scratch_shapes=[
            pltpu.VMEM((FIELDS, 256, LANES), F32),
            pltpu.VMEM((LANES, 256), F32),
            pltpu.VMEM((256, LANES), F32),
            pltpu.VMEM((256, LANES), F32),
            pltpu.VMEM((16, 16, LANES), F32),
            pltpu.VMEM((16, 4) + vreg, F32),
            pltpu.VMEM((16, 32) + vreg, F32),
            pltpu.VMEM((16, 32) + vreg, F32),
            pltpu.VMEM((32,) + vreg, F32),
            pltpu.VMEM((3, 32) + vreg, F32),
            pltpu.VMEM((32,) + vreg, F32),
            pltpu.VMEM((3, 32) + vreg, F32),
            pltpu.VMEM((32,) + vreg, F32),
            pltpu.VMEM((16, 9) + vreg, F32),
            pltpu.VMEM((16, 16, LANES), F32),
            pltpu.VMEM((32, LANES), F32),
            pltpu.VMEM((3, 256, LANES), BF16),
        ],
        compiler_params=params(48),
        name="tiles",
    )(
        tile_perm,
        received,
        tile_order(tile_lists),
        targets[0].transpose(1, 0, 2).reshape(48, 256),
    )
    returned = exchange(returning)
    gsmall, gharm, total_loss = pl.pallas_call(
        functools.partial(splat_back, width_px, height_px),
        out_shape=(shape(11, BLOCKS, LANES), shape(48 * BLOCKS, LANES), shape(1, 1)),
        in_specs=[SM(), VM(), VM(), SM(), VM()],
        out_specs=(VM(), VM(), SM()),
        scratch_shapes=[
            pltpu.VMEM((BLOCKS * TBL, LANES), F32),
            pltpu.VMEM((BLOCKS * LANES + 8, LANES), F32),
            pltpu.VMEM((4, LANES, LANES), F32),
        ],
        compiler_params=params(32),
        name="splat_back",
    )(cam, small, harm, ids, returned)
    flat = gsmall.reshape(11, BLOCKS * LANES)
    rendered = image.reshape(3, 16, 256).transpose(1, 0, 2)[None]
    return (
        rendered,
        total_loss[0, 0],
        flat[0:3],
        flat[3:6],
        flat[6:10],
        flat[10],
        from_tile_order(gharm, 48),
    )


def solution(mesh):
    both = ("view", "pix")
    return jax.shard_map(
        local,
        mesh=mesh,
        in_specs=(
            P(None, both),
            P(None, both),
            P(None, both),
            P(both),
            P(None, both),
            P(),
            P(both, None, None),
            P("pix", None),
            P("pix"),
            P("view", "pix", None, None),
        ),
        out_specs=(
            P("view", "pix", None, None),
            P(),
            P(None, both),
            P(None, both),
            P(None, both),
            P(both),
            P(None, both),
        ),
        check_vma=False,
    )
```

```python
import functools

import jax
import jax.numpy as jnp
from jax import lax
from jax.experimental import pallas as pl
from jax.experimental.pallas import tpu as pltpu
from jax.sharding import PartitionSpec as P

TW = 16
FOCAL = 1100.0
BLUR = 0.3
SH_ZERO = 0.28209479177387814
SH_ONE = 0.4886025119029199
SH_TWO = (
    1.0925484305920792,
    -1.0925484305920792,
    0.31539156525252005,
    -1.0925484305920792,
    0.5462742152960396,
)
SH_THREE = (
    -0.5900435899266435,
    2.890611442640554,
    -0.4570457994644658,
    0.3731763325901154,
    -0.4570457994644658,
    1.445305721320277,
    -0.5900435899266435,
)
LOG2E = 1.4426950408889634
LANES = 128
VIEWS = 4
FIELDS = 9
MSG = 16
TBL = 40
BLOCKS = 64
F32 = jnp.float32
I32 = jnp.int32
BF16 = jnp.bfloat16


def camera_numbers(cameras_ref, cos_ref, sin_ref, cams_ref):
    for view in range(VIEWS):
        numbers = one_camera(cameras_ref, cos_ref, sin_ref, view)
        for i, number in enumerate(numbers):
            cams_ref[view, i] = number


def one_camera(cameras_ref, cos_ref, sin_ref, view):
    ca, cb, cc = [cos_ref[view, i] for i in range(3)]
    sa, sb, sc = [sin_ref[view, i] for i in range(3)]
    turn = [
        [cc * cb, cc * sb * sa - sc * ca, cc * sb * ca + sc * sa],
        [sc * cb, sc * sb * sa + cc * ca, sc * sb * ca - cc * sa],
        [-sb, cb * sa, cb * ca],
    ]
    shift = [cameras_ref[view, 3 + i] for i in range(3)]
    anchor = [-sum(turn[i][e] * shift[i] for i in range(3)) for e in range(3)]
    return turn[0] + turn[1] + turn[2] + shift + anchor


def harmonics(x, y, z):
    xx, yy, zz = x * x, y * y, z * z
    return [
        SH_ZERO * jnp.ones_like(x),
        -SH_ONE * y,
        SH_ONE * z,
        -SH_ONE * x,
        SH_TWO[0] * x * y,
        SH_TWO[1] * y * z,
        SH_TWO[2] * (2.0 * zz - xx - yy),
        SH_TWO[3] * x * z,
        SH_TWO[4] * (xx - yy),
        SH_THREE[0] * y * (3.0 * xx - yy),
        SH_THREE[1] * x * y * z,
        SH_THREE[2] * y * (4.0 * zz - xx - yy),
        SH_THREE[3] * z * (2.0 * zz - 3.0 * xx - 3.0 * yy),
        SH_THREE[4] * x * (4.0 * zz - xx - yy),
        SH_THREE[5] * z * (xx - yy),
        SH_THREE[6] * x * (xx - 3.0 * yy),
    ]


def shape_of(scales, rots):
    inv = 1.0 / jnp.sqrt(sum(q * q for q in rots))
    s, x, y, z = [q * inv for q in rots]
    turn = [
        [1.0 - 2.0 * (y * y + z * z), 2.0 * (x * y - s * z), 2.0 * (x * z + s * y)],
        [2.0 * (x * y + s * z), 1.0 - 2.0 * (x * x + z * z), 2.0 * (y * z - s * x)],
        [2.0 * (x * z - s * y), 2.0 * (y * z + s * x), 1.0 - 2.0 * (x * x + y * y)],
    ]
    spread = [jnp.exp(v) for v in scales]
    m = [[turn[i][e] * spread[e] for e in range(3)] for i in range(3)]
    pairs = ((0, 0), (0, 1), (0, 2), (1, 1), (1, 2), (2, 2))
    return [sum(m[i][e] * m[k][e] for e in range(3)) for i, k in pairs]


def geometry(centers, sigma, cam, width_px, height_px):
    pts = [
        sum(cam[3 * i + e] * centers[e] for e in range(3)) + cam[9 + i] for i in range(3)
    ]
    inv = 1.0 / pts[2]
    diag = FOCAL * inv
    ux, uy = pts[0] * inv, pts[1] * inv
    row_x = [diag * (cam[e] - ux * cam[6 + e]) for e in range(3)]
    row_y = [diag * (cam[3 + e] - uy * cam[6 + e]) for e in range(3)]
    sxx, sxy, sxz, syy, syz, szz = sigma
    full = [[sxx, sxy, sxz], [sxy, syy, syz], [sxz, syz, szz]]
    half_x = [sum(full[i][e] * row_x[e] for e in range(3)) for i in range(3)]
    half_y = [sum(full[i][e] * row_y[e] for e in range(3)) for i in range(3)]
    cov_xx = sum(row_x[i] * half_x[i] for i in range(3)) + BLUR
    cov_xy = sum(row_y[i] * half_x[i] for i in range(3))
    cov_yy = sum(row_y[i] * half_y[i] for i in range(3)) + BLUR
    det = 1.0 / (cov_xx * cov_yy - cov_xy * cov_xy)
    return [
        FOCAL * ux + 0.5 * width_px,
        FOCAL * uy + 0.5 * height_px,
        cov_yy * det,
        -cov_xy * det,
        cov_xx * det,
    ]


def direction_basis(centers, cam):
    off = [centers[e] - cam[12 + e] for e in range(3)]
    inv = 1.0 / jnp.sqrt(sum(v * v for v in off))
    return harmonics(*[v * inv for v in off])


def blocks_of(chunk):
    return pl.ds(pl.multiple_of(chunk * 8, 8), 8)


def load_small(small_ref, chunk):
    some = blocks_of(chunk)
    values = [small_ref[i, some, :] for i in range(11)]
    return values[0:3], values[3:6], values[6:10], jax.nn.sigmoid(values[10])


def harm_slice(row, chunk):
    return pl.ds(((row // 8) * BLOCKS + chunk * 8) * 8 + row % 8, 8, stride=8)


def slot_place(o):
    return (o // 16) * 8 + o % 8, (o // 8) % 2


def splat_out(
    width_px, height_px, cameras_ref, cos_ref, sin_ref,
    small_ref, harm_ref, ids_ref,
    out_ref, last_ref, cams_ref, tbl, by_row, stage,
):
    camera_numbers(cameras_ref, cos_ref, sin_ref, cams_ref)

    def chunk_step(chunk, carry):
        centers, scales, rots, opacity = load_small(small_ref, chunk)
        sigma = shape_of(scales, rots)
        base = chunk * (8 * TBL)
        for view in range(VIEWS):
            cam = [cams_ref[view, i] for i in range(15)]
            record = geometry(centers, sigma, cam, width_px, height_px) + [opacity]
            basis = direction_basis(centers, cam)
            for colour in range(3):
                total = sum(
                    harm_ref[harm_slice(colour * 16 + i, chunk), :] * basis[i]
                    for i in range(16)
                )
                record.append(jnp.maximum(total + 0.5, 0.0))
            for i in range(8):
                tbl[pl.ds(base + view * 8 + i, 8, stride=TBL), :] = record[i]
            tbl[pl.ds(base + 32 + view, 8, stride=TBL), :] = record[8]
        return carry

    lax.fori_loop(0, BLOCKS // 8, chunk_step, 0)

    def turn_step(group, carry):
        for u in range(4):
            b = group * 4 + u
            block = tbl[pl.ds(pl.multiple_of(b * TBL, 8), TBL), :]
            by_row[pl.ds(pl.multiple_of(b * LANES + 8, 8), LANES), 0:TBL] = block.T
        return carry

    lax.fori_loop(0, BLOCKS // 4, turn_step, 0)
    by_row[0:8, :] = jnp.zeros((8, LANES), F32)

    def order_step(group, carry):
        for u in range(4):
            o = group * 4 + u
            for c in range(LANES):
                stage[u, c : c + 1, :] = by_row[pl.ds(ids_ref[o, c], 1), :]
        for u in range(4):
            acc = stage[u, :, 0:TBL].T
            owner, half = slot_place(group * 4 + u)
            for view in range(VIEWS):
                peer = view * 32 + owner
                out_ref[pl.ds(peer * MSG + half, 8, stride=2), :] = acc[view * 8 : view * 8 + 8, :]
                last_ref[pl.ds(peer * 2 + half, 1), :] = acc[32 + view : 33 + view, :]
        return carry

    lax.fori_loop(0, BLOCKS // 4, order_step, 0)


def top_f32(x):
    return x.astype(BF16).astype(F32)


def split(x):
    top = x.astype(BF16)
    return top, x - top.astype(F32)


def product(x, y):
    return jnp.dot(x, y, preferred_element_type=F32)


def summed(x, pattern):
    top, rest = split(x)
    return product(jnp.concatenate([top, rest.astype(BF16)], axis=1), pattern)


def tiles(
    perm_ref, recv_ref, recv_last_ref, list_ref, target_ref,
    out_ref, last_ref, loss_ref, image_ref,
    tab, wide, target_t, image_t, rec, lines, alpha, weight, ends, shades, prefix, res, behind,
    moments, grad, inverse, sums_ref,
):
    lane = lax.broadcasted_iota(I32, (8, LANES), 1)
    sub = lax.broadcasted_iota(I32, (8, LANES), 0)
    sub_f = sub.astype(F32)
    lane_f = lane.astype(F32)
    rows = lax.broadcasted_iota(I32, (LANES, LANES), 0)
    wide_lane = lax.broadcasted_iota(I32, (LANES, LANES), 1)
    tall_lane = lax.broadcasted_iota(I32, (256, LANES), 1)
    from_lane = lax.broadcasted_iota(I32, (256, LANES), 0) % 128
    sums_ref[0] = (from_lane < tall_lane).astype(F32).astype(BF16)
    sums_ref[1] = jnp.ones((256, LANES), BF16)
    sums_ref[2] = (from_lane > tall_lane).astype(F32).astype(BF16)

    for half in range(2):
        for k in range(FIELDS - 1):
            tab[k, half * 128 : half * 128 + 128, :] = recv_ref[
                pl.ds(k * 2 + half, 128, stride=MSG), :
            ].T
        tab[FIELDS - 1, half * 128 : half * 128 + 128, :] = recv_last_ref[
            pl.ds(half, 128, stride=2), :
        ].T
    wide[...] = jnp.zeros_like(wide)
    wide[0:48, :] = target_ref[...]
    for i in range(2):
        target_t[i * 128 : i * 128 + 128, :] = wide[:, i * 128 : i * 128 + 128].T
    image_t[...] = jnp.zeros_like(image_t)

    def take(x, index):
        return jnp.take_along_axis(x, index, axis=1, mode="promise_in_bounds")

    def tile_step(r, carry):
        place = perm_ref[r]
        ox = (16 * (place % TW)).astype(F32)
        oy = (16 * (place // TW)).astype(F32)
        row0 = (r // 8) * 128 + r % 8
        list_lo = list_ref[pl.ds(row0, 8, stride=8), :].astype(F32)
        list_hi = list_ref[pl.ds(row0 + 64, 8, stride=8), :].astype(F32)
        count = jnp.sum(
            (list_lo >= 0.0).astype(F32) + (list_hi >= 0.0).astype(F32)
        ).astype(I32)
        steps = (count + 127) // 128
        pairs = (steps + 1) // 2
        quads = (steps + 3) // 4
        inverse[...] = jnp.zeros_like(inverse)
        tile_rows = pl.multiple_of(r * 16, 8)

        def load_step(group, carry):
            many = [group * 4 + u for u in range(4)]
            entries, masks, records = [], [], []
            for j in many:
                k = lane * steps + j
                block, low = k >> 7, k & 127
                found = jnp.sum(
                    jnp.where(block == sub, take(list_lo, low), 0.0)
                    + jnp.where(block == sub + 8, take(list_hi, low), 0.0),
                    axis=0,
                    keepdims=True,
                ).astype(I32)
                entries.append(jnp.broadcast_to(jnp.where(j < steps, found, -1), (8, LANES)))
            for entry in entries:
                masks.append((entry & 15 == sub, entry & 15 == sub + 8))
                records.append([])
            for f in range(FIELDS):
                half0 = tab[f, pl.ds(tile_rows, 8), :]
                half1 = tab[f, pl.ds(tile_rows + 8, 8), :]
                for entry, (hit0, hit1), fields in zip(entries, masks, records):
                    source = (entry >> 8) & 127
                    got = jnp.where(
                        hit0, take(half0, source), jnp.where(hit1, take(half1, source), 0.0)
                    )
                    fields.append(jnp.sum(got, axis=0, keepdims=True))
            lefts, rights = [], []
            for j, entry, (hit0, hit1) in zip(many, entries, masks):
                listed = entry >= 0
                step_no = (j + 1).astype(F32)
                spots = [jnp.where(listed, step_no, 0.0), jnp.where(listed, lane_f, 0.0)]
                left = [jnp.where(hit, spot, 0.0) for spot in spots for hit in (hit0, hit1)]
                lefts.append(jnp.concatenate(left, axis=0).astype(BF16))
                rights.append((rows == entry[0:1] >> 8).astype(F32).astype(BF16))
            inverse[...] += lax.dot_general(
                jnp.concatenate(lefts, axis=1),
                jnp.concatenate(rights, axis=1),
                (((1,), (1,)), ((), ())),
                preferred_element_type=F32,
            )
            for j, entry, fields in zip(many, entries, records):
                listed = entry[0:1] >= 0
                mx, my = fields[0] - ox, fields[1] - oy
                opacity = jnp.where(listed, fields[5], 1.0)
                level = jnp.where(listed, jnp.log2(opacity), -1e30)
                qyy = (-0.5 * LOG2E) * fields[4]
                values = [mx, my] + fields[2:5] + [opacity] + fields[6:9] + [qyy]
                for i, value in enumerate(values):
                    rec[j, pl.ds(i, 1), :] = value
                qxx = (-0.5 * LOG2E) * fields[2]
                qxy = -LOG2E * fields[3]
                for h in range(2):
                    dx = (sub_f + 8.0 * h) - mx
                    lines[j, 2 * h] = qxy * dx
                    lines[j, 2 * h + 1] = qxx * dx * dx + level
            return carry

        lax.fori_loop(0, quads, load_step, 0)

        def spread(j, i):
            return jnp.broadcast_to(rec[j, pl.ds(i, 1), :], (8, LANES))

        for g in range(4):

            def front_step(pair, carry):
                keep, col = list(carry[:8]), list(carry[8:])
                for j in (pair * 2, pair * 2 + 1):
                    shade = [spread(j, 6 + c) for c in range(3)]
                    my, qyy = spread(j, 1), spread(j, 9)
                    slope = [lines[j, 0], lines[j, 2]]
                    level = [lines[j, 1], lines[j, 3]]
                    for i in range(8):
                        if i % 2 == 0:
                            dy = float(g * 4 + i // 2) - my
                            turn = qyy * dy
                        a = jnp.exp2((slope[i % 2] + turn) * dy + level[i % 2])
                        alpha[j, g * 8 + i] = a
                        w = a * keep[i]
                        weight[j, g * 8 + i] = w
                        keep[i] = keep[i] - w
                        for c in range(3):
                            col[i * 3 + c] = col[i * 3 + c] + shade[c] * w
                return tuple(keep + col)

            start = [jnp.ones((8, LANES), F32)] * 8 + [jnp.zeros((8, LANES), F32)] * 24
            done = lax.fori_loop(0, pairs, front_step, tuple(start))
            for i in range(8):
                ends[g * 8 + i] = done[i]
                for c in range(3):
                    shades[c, g * 8 + i] = done[8 + i * 3 + c]

        for half in range(2):
            part_of = slice(half * 16, half * 16 + 16)
            pixels = slice(half * 128, half * 128 + 128)
            local_end = ends[part_of].reshape(128, LANES)
            top, rest = split(jnp.log2(local_end))
            low = (rest - top_f32(rest)).astype(BF16)
            front = jnp.exp2(
                product(jnp.concatenate([top, rest.astype(BF16)], axis=1), sums_ref[0])
                + product(low, sums_ref[0, 0:128, :])
            )
            prefix[part_of] = front.reshape(16, 8, LANES)
            image = image_t[pixels, :]
            behind_all = jnp.zeros((128, LANES), F32)
            for c in range(3):
                part = front * shades[c, part_of].reshape(128, LANES)
                mine = wide_lane == c * 16 + r
                target = target_t[pixels, :]
                diff = summed(part - jnp.where(mine, target, 0.0), sums_ref[1])
                res[c, part_of] = diff.reshape(16, 8, LANES)
                image = jnp.where(mine, diff + target, image)
                behind_all = behind_all + diff * part
            image_t[pixels, :] = image
            behind[part_of] = (summed(behind_all, sums_ref[2]) / (front * local_end)).reshape(
                16, 8, LANES
            )

        for g in range(4):

            def back_step(back_pair, carry):
                pair = pairs - 1 - back_pair
                return one_back(pair * 2, one_back(pair * 2 + 1, carry))

            def one_back(j, carry):
                back = list(carry)
                shade = [spread(j, 6 + c) for c in range(3)]
                if g == 0:
                    sums = [jnp.zeros((8, LANES), F32)] * 9
                else:
                    sums = [moments[j, i] for i in range(9)]
                for i in range(8):
                    idx = g * 8 + i
                    h = i % 2
                    a = alpha[j, idx]
                    w = weight[j, idx] * prefix[idx]
                    diff = [res[c, idx] for c in range(3)]
                    u = shade[0] * diff[0] + shade[1] * diff[1] + shade[2] * diff[2] - back[i]
                    back[i] = back[i] + a * u
                    v = w * u
                    for c in range(3):
                        sums[6 + c] = sums[6 + c] + diff[c] * w
                    sums[3 * h] = sums[3 * h] + v
                    sums[3 * h + 1] = sums[3 * h + 1] + sums[3 * h]
                    sums[3 * h + 2] = sums[3 * h + 2] + sums[3 * h + 1]
                for i in range(9):
                    moments[j, i] = sums[i]
                return tuple(back)

            lax.fori_loop(0, pairs, back_step, tuple(behind[g * 8 + i] for i in range(8)))

        def finish_step(group, carry):
            for u in range(4):
                finish(group * 4 + u)
            return carry

        def finish(j):
            def total(x):
                return jnp.sum(x, axis=0, keepdims=True)

            s = [moments[j, i] for i in range(9)]
            x0, x1 = sub_f, sub_f + 8.0
            y1 = [16.0 * s[3 * h] - s[3 * h + 1] for h in range(2)]
            y2 = [256.0 * s[3 * h] - 33.0 * s[3 * h + 1] + 2.0 * s[3 * h + 2] for h in range(2)]
            m0 = total(s[0] + s[3])
            m_x = total(x0 * s[0] + x1 * s[3])
            m_xx = total(x0 * x0 * s[0] + x1 * x1 * s[3])
            m_y = total(y1[0] + y1[1])
            m_xy = total(x0 * y1[0] + x1 * y1[1])
            m_yy = total(y2[0] + y2[1])
            mx, my, xx, xy, yy, opacity = [rec[j, pl.ds(i, 1), :] for i in range(6)]
            g_x = m_x - mx * m0
            g_y = m_y - my * m0
            g_xx = m_xx - 2.0 * mx * m_x + mx * mx * m0
            g_xy = m_xy - mx * m_y - my * m_x + mx * my * m0
            g_yy = m_yy - 2.0 * my * m_y + my * my * m0
            out = [
                xx * g_x + xy * g_y,
                yy * g_y + xy * g_x,
                -0.5 * g_xx,
                -g_xy,
                -0.5 * g_yy,
                m0 / opacity,
            ] + [total(s[6 + c]) for c in range(3)]
            for i in range(FIELDS):
                grad[j, pl.ds(i, 1), :] = out[i]

        lax.fori_loop(0, quads, finish_step, 0)

        step0 = inverse[0:8, :].astype(I32)
        step1 = inverse[8:16, :].astype(I32)
        lane0 = inverse[16:24, :].astype(I32)
        lane1 = inverse[24:32, :].astype(I32)

        def unlist_step(group, carry):
            acc = list(carry)
            for j in [group * 4 + u for u in range(4)]:
                hit0, hit1 = step0 == j + 1, step1 == j + 1
                for f in range(FIELDS):
                    row = jnp.broadcast_to(grad[j, pl.ds(f, 1), :], (8, LANES))
                    acc[2 * f] = jnp.where(hit0, take(row, lane0), acc[2 * f])
                    acc[2 * f + 1] = jnp.where(hit1, take(row, lane1), acc[2 * f + 1])
            return tuple(acc)

        acc = lax.fori_loop(0, quads, unlist_step, (jnp.zeros((8, LANES), F32),) * 18)
        for f in range(FIELDS):
            tab[f, pl.ds(tile_rows, 8), :] = acc[2 * f]
            tab[f, pl.ds(tile_rows + 8, 8), :] = acc[2 * f + 1]
        return carry

    lax.fori_loop(0, 16, tile_step, 0)
    errors = image_t[...] - target_t[...]
    total = jnp.sum(errors * errors, axis=0, keepdims=True)
    loss_ref[...] = jnp.broadcast_to(total, (128, LANES))
    for half in range(2):
        for k in range(FIELDS - 1):
            out_ref[pl.ds(k * 2 + half, 128, stride=MSG), :] = tab[
                k, half * 128 : half * 128 + 128, :
            ].T
        last_ref[pl.ds(half, 128, stride=2), :] = tab[
            FIELDS - 1, half * 128 : half * 128 + 128, :
        ].T
    for i in range(2):
        wide[:, i * 128 : i * 128 + 128] = image_t[i * 128 : i * 128 + 128, :].T
    image_ref[...] = wide[0:48, :]


def splat_back(
    width_px, height_px, cameras_ref, cos_ref, sin_ref,
    small_ref, harm_ref, ids_ref,
    ret_ref, ret_last_ref, losses_ref,
    gsmall_ref, gharm_ref, loss_ref,
    cams_ref, nat, by_row, stage,
):
    camera_numbers(cameras_ref, cos_ref, sin_ref, cams_ref)
    losses = jnp.sum(losses_ref[...], axis=0, keepdims=True)
    loss_ref[0, 0] = 0.5 * jnp.sum(losses)

    def clear_step(b, carry):
        by_row[pl.ds(pl.multiple_of(b * LANES + 8, 8), LANES), :] = jnp.zeros((LANES, LANES), F32)
        return carry

    lax.fori_loop(0, BLOCKS, clear_step, 0)

    def order_step(group, carry):
        for u in range(4):
            owner, half = slot_place(group * 4 + u)
            peers = [view * 32 + owner for view in range(VIEWS)]
            parts = [ret_ref[pl.ds(peer * MSG + half, 8, stride=2), :] for peer in peers]
            parts += [ret_last_ref[pl.ds(peer * 2 + half, 1), :] for peer in peers]
            parts.append(jnp.zeros((4, LANES), F32))
            stage[u, :, 0:TBL] = jnp.concatenate(parts, axis=0).T
        for u in range(4):
            for c in range(LANES):
                by_row[pl.ds(ids_ref[group * 4 + u, c], 1), :] = stage[u, c : c + 1, :]
        return carry

    lax.fori_loop(0, BLOCKS // 4, order_step, 0)

    def turn_step(group, carry):
        for u in range(4):
            n = group * 4 + u
            block = by_row[pl.ds(pl.multiple_of(n * LANES + 8, 8), LANES), 0:TBL].T
            for i in range(5):
                nat[pl.ds(8 * i * BLOCKS + n, 8, stride=BLOCKS), :] = block[8 * i : 8 * i + 8, :]
        return carry

    lax.fori_loop(0, BLOCKS // 4, turn_step, 0)

    def chunk_step(chunk, carry):
        centers, scales, rots, opacity = load_small(small_ref, chunk)

        def given(view, i):
            row = view * 8 + i if i < 8 else 32 + view
            return nat[pl.ds(pl.multiple_of(row * BLOCKS + chunk * 8, 8), 8), :]

        sigma, shape_pull = jax.vjp(shape_of, scales, rots)
        d_centers = [jnp.zeros((8, LANES), F32)] * 3
        d_sigma = [jnp.zeros((8, LANES), F32)] * 6
        d_opacity = jnp.zeros((8, LANES), F32)
        for view in range(VIEWS):
            cam = [cams_ref[view, i] for i in range(15)]
            _, geo_pull = jax.vjp(
                lambda c, s: geometry(c, s, cam, width_px, height_px), centers, sigma
            )
            d_c, d_s = geo_pull([given(view, i) for i in range(5)])
            basis, dir_pull = jax.vjp(lambda c: direction_basis(c, cam), centers)
            d_opacity = d_opacity + given(view, 5)
            d_basis = [jnp.zeros((8, LANES), F32)] * 16
            for colour in range(3):
                rows = [harm_slice(colour * 16 + i, chunk) for i in range(16)]
                coeffs = [harm_ref[row, :] for row in rows]
                total = sum(coeffs[i] * basis[i] for i in range(16)) + 0.5
                slope = jnp.where(total > 0.0, 1.0, jnp.where(total == 0.0, 0.5, 0.0))
                d_total = given(view, 6 + colour) * slope
                for i in range(16):
                    d_basis[i] = d_basis[i] + d_total * coeffs[i]
                    term = d_total * basis[i]
                    if view == 0:
                        gharm_ref[rows[i], :] = term
                    else:
                        gharm_ref[rows[i], :] = gharm_ref[rows[i], :] + term
            (d_dir,) = dir_pull(d_basis)
            d_centers = [d_centers[e] + d_c[e] + d_dir[e] for e in range(3)]
            d_sigma = [d_sigma[e] + d_s[e] for e in range(6)]
        d_scales, d_rots = shape_pull(d_sigma)
        some = blocks_of(chunk)
        values = list(d_centers) + list(d_scales) + list(d_rots)
        values.append(d_opacity * opacity * (1.0 - opacity))
        for i, value in enumerate(values):
            gsmall_ref[i, some, :] = value
        return carry

    lax.fori_loop(0, BLOCKS // 8, chunk_step, 0)


def tile_order(x):
    rows, width = x.shape
    split = x.reshape(rows // 8, 8, width // LANES, LANES)
    return split.transpose(0, 2, 1, 3).reshape(rows * width // LANES, LANES)


def from_tile_order(x, rows):
    width = x.shape[0] * LANES // rows
    split = x.reshape(rows // 8, width // LANES, 8, LANES)
    return split.transpose(0, 2, 1, 3).reshape(rows, width)


def params(mib):
    return pltpu.CompilerParams(vmem_limit_bytes=mib * 1024 * 1024)


def shape(*dims):
    return jax.ShapeDtypeStruct(dims, F32)


VM = functools.partial(pl.BlockSpec, memory_space=pltpu.VMEM)
SM = functools.partial(pl.BlockSpec, memory_space=pltpu.SMEM)


def exchange_kernel(count, *refs):
    sources, places = refs[:count], refs[count : 2 * count]
    sent, arrived, own = refs[2 * count :]
    view, pix = lax.axis_index("view"), lax.axis_index("pix")
    me = view * 32 + pix
    kept = [
        pltpu.make_async_copy(sources[i].at[me], places[i].at[me], own.at[i])
        for i in range(count)
    ]
    for copy in kept:
        copy.start()

    def send(step, carry):
        peer = lax.rem(me + step, 128)
        for i in range(count):
            pltpu.make_async_remote_copy(
                src_ref=sources[i].at[peer],
                dst_ref=places[i].at[me],
                send_sem=sent.at[i],
                recv_sem=arrived.at[i],
                device_id=(peer // 32, lax.rem(peer, 32)),
                device_id_type=pl.DeviceIdType.MESH,
            ).start()
        return carry

    lax.fori_loop(1, 128, send, 0)
    for copy in kept:
        copy.wait()
    for i in range(count):
        pltpu.make_async_remote_copy(
            src_ref=sources[i].at[pl.ds(0, 127)],
            dst_ref=places[i].at[pl.ds(0, 127)],
            send_sem=sent.at[i],
            recv_sem=arrived.at[i],
            device_id=(view, lax.rem(pix + 1, 32)),
            device_id_type=pl.DeviceIdType.MESH,
        ).wait()


def exchange(*messages):
    count = len(messages)
    blocks = [m.reshape(128, m.shape[0] // 128, LANES) for m in messages]
    outs = pl.pallas_call(
        functools.partial(exchange_kernel, count),
        out_shape=tuple(shape(*b.shape) for b in blocks),
        in_specs=[VM()] * count,
        out_specs=(VM(),) * count,
        scratch_shapes=[pltpu.SemaphoreType.DMA((count,))] * 3,
        compiler_params=pltpu.CompilerParams(
            has_side_effects=True, vmem_limit_bytes=16 * 1024 * 1024
        ),
        name="exchange",
    )(*blocks)
    return [out.reshape(m.shape) for out, m in zip(outs, messages)]


def local(
    centers, log_scales, rotations, logits, harmonic_coeffs,
    cameras, send_ids, tile_lists, tile_perm, targets,
):
    width_px = 16 * TW
    height_px = 16 * (512 // TW)
    views = (cameras, jnp.cos(cameras[:, :3]), jnp.sin(cameras[:, :3]))
    small = jnp.concatenate([centers, log_scales, rotations, logits[None]], axis=0)
    small = small.reshape(11, BLOCKS, LANES)
    harm = tile_order(harmonic_coeffs)
    ids = tile_order(send_ids[0]) + 8
    sending, sending_last = pl.pallas_call(
        functools.partial(splat_out, width_px, height_px),
        out_shape=(shape(128 * MSG, LANES), shape(256, LANES)),
        in_specs=[SM()] * 3 + [VM()] * 2 + [SM()],
        out_specs=(VM(), VM()),
        scratch_shapes=[
            pltpu.SMEM((VIEWS, 16), F32),
            pltpu.VMEM((BLOCKS * TBL, LANES), F32),
            pltpu.VMEM((BLOCKS * LANES + 8, LANES), F32),
            pltpu.VMEM((4, LANES, LANES), F32),
        ],
        compiler_params=params(32),
        name="splat_out",
    )(*views, small, harm, ids)
    received = exchange(sending, sending_last)
    vreg = (8, LANES)
    *returning, image = pl.pallas_call(
        tiles,
        out_shape=(
            shape(128 * MSG, LANES), shape(256, LANES), shape(128, LANES), shape(48, 256),
        ),
        in_specs=[SM(), VM(), VM(), VM(), VM()],
        out_specs=(VM(), VM(), VM(), VM()),
        scratch_shapes=[
            pltpu.VMEM((FIELDS, 256, LANES), F32),
            pltpu.VMEM((LANES, 256), F32),
            pltpu.VMEM((256, LANES), F32),
            pltpu.VMEM((256, LANES), F32),
            pltpu.VMEM((16, 16, LANES), F32),
            pltpu.VMEM((16, 4) + vreg, F32),
            pltpu.VMEM((16, 32) + vreg, F32),
            pltpu.VMEM((16, 32) + vreg, F32),
            pltpu.VMEM((32,) + vreg, F32),
            pltpu.VMEM((3, 32) + vreg, F32),
            pltpu.VMEM((32,) + vreg, F32),
            pltpu.VMEM((3, 32) + vreg, F32),
            pltpu.VMEM((32,) + vreg, F32),
            pltpu.VMEM((16, 9) + vreg, F32),
            pltpu.VMEM((16, 16, LANES), F32),
            pltpu.VMEM((32, LANES), F32),
            pltpu.VMEM((3, 256, LANES), BF16),
        ],
        compiler_params=params(48),
        name="tiles",
    )(
        tile_perm,
        *received,
        tile_order(tile_lists),
        targets[0].transpose(1, 0, 2).reshape(48, 256),
    )
    returned = exchange(*returning)
    gsmall, gharm, total_loss = pl.pallas_call(
        functools.partial(splat_back, width_px, height_px),
        out_shape=(shape(11, BLOCKS, LANES), shape(48 * BLOCKS, LANES), shape(1, 1)),
        in_specs=[SM()] * 3 + [VM()] * 2 + [SM()] + [VM()] * 3,
        out_specs=(VM(), VM(), SM()),
        scratch_shapes=[
            pltpu.SMEM((VIEWS, 16), F32),
            pltpu.VMEM((BLOCKS * TBL, LANES), F32),
            pltpu.VMEM((BLOCKS * LANES + 8, LANES), F32),
            pltpu.VMEM((4, LANES, LANES), F32),
        ],
        compiler_params=params(32),
        name="splat_back",
    )(*views, small, harm, ids, *returned)
    flat = gsmall.reshape(11, BLOCKS * LANES)
    rendered = image.reshape(3, 16, 256).transpose(1, 0, 2)[None]
    return (
        rendered,
        total_loss[0, 0],
        flat[0:3],
        flat[3:6],
        flat[6:10],
        flat[10],
        from_tile_order(gharm, 48),
    )


def solution(mesh):
    both = ("view", "pix")
    return jax.shard_map(
        local,
        mesh=mesh,
        in_specs=(
            P(None, both),
            P(None, both),
            P(None, both),
            P(both),
            P(None, both),
            P(),
            P(both, None, None),
            P("pix", None),
            P("pix"),
            P("view", "pix", None, None),
        ),
        out_specs=(
            P("view", "pix", None, None),
            P(),
            P(None, both),
            P(None, both),
            P(None, both),
            P(both),
            P(None, both),
        ),
        check_vma=False,
    )
```

```python
import functools

import jax
import jax.numpy as jnp
from jax import lax
from jax.experimental import pallas as pl
from jax.experimental.pallas import tpu as pltpu
from jax.sharding import PartitionSpec as P

TW = 16
FOCAL = 1100.0
BLUR = 0.3
SH_ZERO = 0.28209479177387814
SH_ONE = 0.4886025119029199
SH_TWO = (
    1.0925484305920792,
    -1.0925484305920792,
    0.31539156525252005,
    -1.0925484305920792,
    0.5462742152960396,
)
SH_THREE = (
    -0.5900435899266435,
    2.890611442640554,
    -0.4570457994644658,
    0.3731763325901154,
    -0.4570457994644658,
    1.445305721320277,
    -0.5900435899266435,
)
LOG2E = 1.4426950408889634
LANES = 128
VIEWS = 4
FIELDS = 9
MSG = 16
TBL = 40
BLOCKS = 64
F32 = jnp.float32
I32 = jnp.int32
BF16 = jnp.bfloat16


def camera_numbers(cameras_ref, cos_ref, sin_ref, cams_ref):
    for view in range(VIEWS):
        numbers = one_camera(cameras_ref, cos_ref, sin_ref, view)
        for i, number in enumerate(numbers):
            cams_ref[view, i] = number


def one_camera(cameras_ref, cos_ref, sin_ref, view):
    ca, cb, cc = [cos_ref[view, i] for i in range(3)]
    sa, sb, sc = [sin_ref[view, i] for i in range(3)]
    turn = [
        [cc * cb, cc * sb * sa - sc * ca, cc * sb * ca + sc * sa],
        [sc * cb, sc * sb * sa + cc * ca, sc * sb * ca - cc * sa],
        [-sb, cb * sa, cb * ca],
    ]
    shift = [cameras_ref[view, 3 + i] for i in range(3)]
    anchor = [-sum(turn[i][e] * shift[i] for i in range(3)) for e in range(3)]
    return turn[0] + turn[1] + turn[2] + shift + anchor


def harmonics(x, y, z):
    xx, yy, zz = x * x, y * y, z * z
    return [
        SH_ZERO * jnp.ones_like(x),
        -SH_ONE * y,
        SH_ONE * z,
        -SH_ONE * x,
        SH_TWO[0] * x * y,
        SH_TWO[1] * y * z,
        SH_TWO[2] * (2.0 * zz - xx - yy),
        SH_TWO[3] * x * z,
        SH_TWO[4] * (xx - yy),
        SH_THREE[0] * y * (3.0 * xx - yy),
        SH_THREE[1] * x * y * z,
        SH_THREE[2] * y * (4.0 * zz - xx - yy),
        SH_THREE[3] * z * (2.0 * zz - 3.0 * xx - 3.0 * yy),
        SH_THREE[4] * x * (4.0 * zz - xx - yy),
        SH_THREE[5] * z * (xx - yy),
        SH_THREE[6] * x * (xx - 3.0 * yy),
    ]


def shape_of(scales, rots):
    inv = 1.0 / jnp.sqrt(sum(q * q for q in rots))
    s, x, y, z = [q * inv for q in rots]
    turn = [
        [1.0 - 2.0 * (y * y + z * z), 2.0 * (x * y - s * z), 2.0 * (x * z + s * y)],
        [2.0 * (x * y + s * z), 1.0 - 2.0 * (x * x + z * z), 2.0 * (y * z - s * x)],
        [2.0 * (x * z - s * y), 2.0 * (y * z + s * x), 1.0 - 2.0 * (x * x + y * y)],
    ]
    spread = [jnp.exp(v) for v in scales]
    m = [[turn[i][e] * spread[e] for e in range(3)] for i in range(3)]
    pairs = ((0, 0), (0, 1), (0, 2), (1, 1), (1, 2), (2, 2))
    return [sum(m[i][e] * m[k][e] for e in range(3)) for i, k in pairs]


def geometry(centers, sigma, cam, width_px, height_px):
    pts = [
        sum(cam[3 * i + e] * centers[e] for e in range(3)) + cam[9 + i] for i in range(3)
    ]
    inv = 1.0 / pts[2]
    diag = FOCAL * inv
    ux, uy = pts[0] * inv, pts[1] * inv
    row_x = [diag * (cam[e] - ux * cam[6 + e]) for e in range(3)]
    row_y = [diag * (cam[3 + e] - uy * cam[6 + e]) for e in range(3)]
    sxx, sxy, sxz, syy, syz, szz = sigma
    full = [[sxx, sxy, sxz], [sxy, syy, syz], [sxz, syz, szz]]
    half_x = [sum(full[i][e] * row_x[e] for e in range(3)) for i in range(3)]
    half_y = [sum(full[i][e] * row_y[e] for e in range(3)) for i in range(3)]
    cov_xx = sum(row_x[i] * half_x[i] for i in range(3)) + BLUR
    cov_xy = sum(row_y[i] * half_x[i] for i in range(3))
    cov_yy = sum(row_y[i] * half_y[i] for i in range(3)) + BLUR
    det = 1.0 / (cov_xx * cov_yy - cov_xy * cov_xy)
    return [
        FOCAL * ux + 0.5 * width_px,
        FOCAL * uy + 0.5 * height_px,
        cov_yy * det,
        -cov_xy * det,
        cov_xx * det,
    ]


def direction_basis(centers, cam):
    off = [centers[e] - cam[12 + e] for e in range(3)]
    inv = 1.0 / jnp.sqrt(sum(v * v for v in off))
    return harmonics(*[v * inv for v in off])


def load_small(small_ref, chunk):
    some = pl.ds(pl.multiple_of(chunk * 8, 8), 8)
    values = [small_ref[i, some, :] for i in range(11)]
    return values[0:3], values[3:6], values[6:10], jax.nn.sigmoid(values[10])


def harm_slice(row, chunk):
    return pl.ds(((row // 8) * BLOCKS + chunk * 8) * 8 + row % 8, 8, stride=8)


def slot_place(o):
    return (o // 16) * 8 + o % 8, (o // 8) % 2


def alternate(fill, drain, stage_a, stage_b):
    groups = BLOCKS // 2
    fill(stage_a, 0)

    def step(pair, carry):
        fill(stage_b, pair * 2 + 1)
        drain(stage_a, pair * 2)
        fill(stage_a, jnp.minimum(pair * 2 + 2, groups - 1))
        drain(stage_b, pair * 2 + 1)
        return carry

    lax.fori_loop(0, groups // 2, step, 0)


def splat_out(
    width_px, height_px, cameras_ref, cos_ref, sin_ref,
    small_ref, harm_ref, ids_ref,
    out_ref, last_ref, cams_ref, tbl, by_row, stage_a, stage_b,
):
    camera_numbers(cameras_ref, cos_ref, sin_ref, cams_ref)

    def chunk_step(chunk, carry):
        centers, scales, rots, opacity = load_small(small_ref, chunk)
        sigma = shape_of(scales, rots)
        base = chunk * (8 * TBL)
        for view in range(VIEWS):
            cam = [cams_ref[view, i] for i in range(15)]
            record = geometry(centers, sigma, cam, width_px, height_px) + [opacity]
            basis = direction_basis(centers, cam)
            for colour in range(3):
                total = sum(
                    harm_ref[harm_slice(colour * 16 + i, chunk), :] * basis[i]
                    for i in range(16)
                )
                record.append(jnp.maximum(total + 0.5, 0.0))
            for i in range(8):
                tbl[pl.ds(base + view * 8 + i, 8, stride=TBL), :] = record[i]
            tbl[pl.ds(base + 32 + view, 8, stride=TBL), :] = record[8]
        return carry

    lax.fori_loop(0, BLOCKS // 8, chunk_step, 0)

    def turn_step(group, carry):
        for u in range(4):
            b = group * 4 + u
            block = tbl[pl.ds(pl.multiple_of(b * TBL, 8), TBL), :]
            by_row[pl.ds(pl.multiple_of(b * LANES + 8, 8), LANES), 0:TBL] = block.T
        return carry

    lax.fori_loop(0, BLOCKS // 4, turn_step, 0)
    by_row[0:8, :] = jnp.zeros((8, LANES), F32)

    def fill(stage, group):
        for u in range(2):
            for c in range(LANES):
                stage[u, c : c + 1, :] = by_row[pl.ds(ids_ref[group * 2 + u, c] + 8, 1), :]

    def drain(stage, group):
        for u in range(2):
            acc = stage[u, :, 0:TBL].T
            owner, half = slot_place(group * 2 + u)
            for view in range(VIEWS):
                peer = view * 32 + owner
                out_ref[pl.ds(peer * MSG + half, 8, stride=2), :] = acc[view * 8 : view * 8 + 8, :]
                last_ref[pl.ds(peer * 2 + half, 1), :] = acc[32 + view : 33 + view, :]

    alternate(fill, drain, stage_a, stage_b)


def top_f32(x):
    return x.astype(BF16).astype(F32)


def split(x):
    top = x.astype(BF16)
    return top, x - top.astype(F32)


def product(x, y):
    return jnp.dot(x, y, preferred_element_type=F32)


def summed(x, pattern):
    top, rest = split(x)
    return product(jnp.concatenate([top, rest.astype(BF16)], axis=1), pattern)


def tiles(
    perm_ref, recv_ref, recv_last_ref, list_ref, target_ref,
    out_ref, last_ref, loss_ref, image_ref,
    tab, wide, target_t, image_t, rec, lines, alpha, weight, ends, shades, prefix, res, behind,
    moments, grad, inverse, sums_ref,
):
    lane = lax.broadcasted_iota(I32, (8, LANES), 1)
    sub = lax.broadcasted_iota(I32, (8, LANES), 0)
    sub_f = sub.astype(F32)
    lane_f = lane.astype(F32)
    rows = lax.broadcasted_iota(I32, (LANES, LANES), 0)
    tall_lane = lax.broadcasted_iota(I32, (256, LANES), 1)
    from_lane = lax.broadcasted_iota(I32, (256, LANES), 0) % 128
    sums_ref[0] = (from_lane < tall_lane).astype(F32).astype(BF16)
    sums_ref[1] = jnp.ones((256, LANES), BF16)
    sums_ref[2] = (from_lane > tall_lane).astype(F32).astype(BF16)

    for half in range(2):
        for k in range(FIELDS - 1):
            tab[k, half * 128 : half * 128 + 128, :] = recv_ref[
                pl.ds(k * 2 + half, 128, stride=MSG), :
            ].T
        tab[FIELDS - 1, half * 128 : half * 128 + 128, :] = recv_last_ref[
            pl.ds(half, 128, stride=2), :
        ].T
    wide[...] = jnp.zeros_like(wide)
    wide[0:48, :] = target_ref[...]
    for i in range(2):
        target_t[i * 128 : i * 128 + 128, :] = wide[:, i * 128 : i * 128 + 128].T
    image_t[...] = jnp.zeros_like(image_t)

    def take(x, index):
        return jnp.take_along_axis(x, index, axis=1, mode="promise_in_bounds")

    def tile_step(r, carry):
        place = perm_ref[r]
        ox = (16 * (place % TW)).astype(F32)
        oy = (16 * (place // TW)).astype(F32)
        row0 = (r // 8) * 128 + r % 8
        list_lo = list_ref[pl.ds(row0, 8, stride=8), :].astype(F32)
        list_hi = list_ref[pl.ds(row0 + 64, 8, stride=8), :].astype(F32)
        count = jnp.sum(
            (list_lo >= 0.0).astype(F32) + (list_hi >= 0.0).astype(F32)
        ).astype(I32)
        steps = (count + 127) // 128
        pairs = (steps + 1) // 2
        quads = (steps + 3) // 4
        inverse[...] = jnp.zeros_like(inverse)
        tile_rows = pl.multiple_of(r * 16, 8)

        def load_step(group, carry):
            many = [group * 4 + u for u in range(4)]
            entries, masks, records = [], [], []
            for j in many:
                k = lane * steps + j
                block, low = k >> 7, k & 127
                found = jnp.sum(
                    jnp.where(block == sub, take(list_lo, low), 0.0)
                    + jnp.where(block == sub + 8, take(list_hi, low), 0.0),
                    axis=0,
                    keepdims=True,
                ).astype(I32)
                entries.append(jnp.broadcast_to(jnp.where(j < steps, found, -1), (8, LANES)))
            for entry in entries:
                masks.append((entry & 15 == sub, entry & 15 == sub + 8))
                records.append([])
            for f in range(FIELDS):
                half0 = tab[f, pl.ds(tile_rows, 8), :]
                half1 = tab[f, pl.ds(tile_rows + 8, 8), :]
                for entry, (hit0, hit1), fields in zip(entries, masks, records):
                    source = (entry >> 8) & 127
                    got = jnp.where(
                        hit0, take(half0, source), jnp.where(hit1, take(half1, source), 0.0)
                    )
                    fields.append(jnp.sum(got, axis=0, keepdims=True))
            lefts, rights = [], []
            for j, entry, (hit0, hit1) in zip(many, entries, masks):
                listed = entry >= 0
                step_no = (j + 1).astype(F32)
                spots = [jnp.where(listed, step_no, 0.0), jnp.where(listed, lane_f, 0.0)]
                left = [jnp.where(hit, spot, 0.0) for spot in spots for hit in (hit0, hit1)]
                lefts.append(jnp.concatenate(left, axis=0).astype(BF16))
                rights.append((rows == entry[0:1] >> 8).astype(F32).astype(BF16))
            inverse[...] += lax.dot_general(
                jnp.concatenate(lefts, axis=1),
                jnp.concatenate(rights, axis=1),
                (((1,), (1,)), ((), ())),
                preferred_element_type=F32,
            )
            for j, entry, fields in zip(many, entries, records):
                listed = entry[0:1] >= 0
                mx, my = fields[0] - ox, fields[1] - oy
                opacity = jnp.where(listed, fields[5], 1.0)
                level = jnp.where(listed, jnp.log2(opacity), -1e30)
                qyy = (-0.5 * LOG2E) * fields[4]
                values = [mx, my] + fields[2:5] + [opacity] + fields[6:9] + [qyy]
                for i, value in enumerate(values):
                    rec[j, pl.ds(i, 1), :] = value
                qxx = (-0.5 * LOG2E) * fields[2]
                qxy = -LOG2E * fields[3]
                for h in range(2):
                    dx = (sub_f + 8.0 * h) - mx
                    lines[j, 2 * h] = qxy * dx
                    lines[j, 2 * h + 1] = qxx * dx * dx + level
            return carry

        lax.fori_loop(0, quads, load_step, 0)

        def spread(j, i):
            return jnp.broadcast_to(rec[j, pl.ds(i, 1), :], (8, LANES))

        for g in range(4):

            def front_step(pair, carry):
                keep, col = list(carry[:8]), list(carry[8:])
                for j in (pair * 2, pair * 2 + 1):
                    shade = [spread(j, 6 + c) for c in range(3)]
                    my, qyy = spread(j, 1), spread(j, 9)
                    slope = [lines[j, 0], lines[j, 2]]
                    level = [lines[j, 1], lines[j, 3]]
                    for i in range(8):
                        if i % 2 == 0:
                            dy = float(g * 4 + i // 2) - my
                            turn = qyy * dy
                        a = jnp.exp2((slope[i % 2] + turn) * dy + level[i % 2])
                        alpha[j, g * 8 + i] = a
                        w = a * keep[i]
                        weight[j, g * 8 + i] = w
                        keep[i] = keep[i] - w
                        for c in range(3):
                            col[i * 3 + c] = col[i * 3 + c] + shade[c] * w
                return tuple(keep + col)

            start = [jnp.ones((8, LANES), F32)] * 8 + [jnp.zeros((8, LANES), F32)] * 24
            done = lax.fori_loop(0, pairs, front_step, tuple(start))
            for i in range(8):
                ends[g * 8 + i] = done[i]
                for c in range(3):
                    shades[c, g * 8 + i] = done[8 + i * 3 + c]

        local_end = ends[...].reshape(256, LANES)
        top, rest = split(jnp.log2(local_end))
        low = (rest - top_f32(rest)).astype(BF16)
        front = jnp.exp2(
            product(jnp.concatenate([top, rest.astype(BF16)], axis=1), sums_ref[0])
            + product(low, sums_ref[0, 0:128, :])
        )
        prefix[...] = front.reshape(32, 8, LANES)
        parts = [front * shades[c].reshape(256, LANES) for c in range(3)]
        target = target_t[...]
        masks = [tall_lane == c * 16 + r for c in range(3)]
        diffs = [
            jnp.sum(part - jnp.where(mine, target, 0.0), axis=1, keepdims=True)
            for part, mine in zip(parts, masks)
        ]
        image = image_t[...]
        behind_all = jnp.zeros((256, LANES), F32)
        for c in range(3):
            diff = jnp.broadcast_to(diffs[c], (256, LANES))
            res[c] = diff.reshape(32, 8, LANES)
            image = jnp.where(masks[c], diff + target, image)
            behind_all = behind_all + diff * parts[c]
        image_t[...] = image
        behind[...] = (summed(behind_all, sums_ref[2]) / (front * local_end)).reshape(
            32, 8, LANES
        )

        for g in range(4):

            def back_step(back_pair, carry):
                pair = pairs - 1 - back_pair
                return one_back(pair * 2, one_back(pair * 2 + 1, carry))

            def one_back(j, carry):
                back = list(carry)
                shade = [spread(j, 6 + c) for c in range(3)]
                if g == 0:
                    sums = [jnp.zeros((8, LANES), F32)] * 9
                else:
                    sums = [moments[j, i] for i in range(9)]
                for i in range(8):
                    idx = g * 8 + i
                    h = i % 2
                    a = alpha[j, idx]
                    w = weight[j, idx] * prefix[idx]
                    diff = [res[c, idx] for c in range(3)]
                    u = shade[0] * diff[0] + shade[1] * diff[1] + shade[2] * diff[2] - back[i]
                    back[i] = back[i] + a * u
                    v = w * u
                    for c in range(3):
                        sums[6 + c] = sums[6 + c] + diff[c] * w
                    sums[3 * h] = sums[3 * h] + v
                    sums[3 * h + 1] = sums[3 * h + 1] + sums[3 * h]
                    sums[3 * h + 2] = sums[3 * h + 2] + sums[3 * h + 1]
                for i in range(9):
                    moments[j, i] = sums[i]
                return tuple(back)

            lax.fori_loop(0, pairs, back_step, tuple(behind[g * 8 + i] for i in range(8)))

        def finish_step(group, carry):
            for u in range(4):
                finish(group * 4 + u)
            return carry

        def finish(j):
            def total(x):
                return jnp.sum(x, axis=0, keepdims=True)

            s = [moments[j, i] for i in range(9)]
            x0, x1 = sub_f, sub_f + 8.0
            y1 = [16.0 * s[3 * h] - s[3 * h + 1] for h in range(2)]
            y2 = [256.0 * s[3 * h] - 33.0 * s[3 * h + 1] + 2.0 * s[3 * h + 2] for h in range(2)]
            m0 = total(s[0] + s[3])
            m_x = total(x0 * s[0] + x1 * s[3])
            m_xx = total(x0 * x0 * s[0] + x1 * x1 * s[3])
            m_y = total(y1[0] + y1[1])
            m_xy = total(x0 * y1[0] + x1 * y1[1])
            m_yy = total(y2[0] + y2[1])
            mx, my, xx, xy, yy, opacity = [rec[j, pl.ds(i, 1), :] for i in range(6)]
            g_x = m_x - mx * m0
            g_y = m_y - my * m0
            g_xx = m_xx - 2.0 * mx * m_x + mx * mx * m0
            g_xy = m_xy - mx * m_y - my * m_x + mx * my * m0
            g_yy = m_yy - 2.0 * my * m_y + my * my * m0
            out = [
                xx * g_x + xy * g_y,
                yy * g_y + xy * g_x,
                -0.5 * g_xx,
                -g_xy,
                -0.5 * g_yy,
                m0 / opacity,
            ] + [total(s[6 + c]) for c in range(3)]
            for i in range(FIELDS):
                grad[j, pl.ds(i, 1), :] = out[i]

        lax.fori_loop(0, quads, finish_step, 0)

        step0 = inverse[0:8, :].astype(I32)
        step1 = inverse[8:16, :].astype(I32)
        lane0 = inverse[16:24, :].astype(I32)
        lane1 = inverse[24:32, :].astype(I32)

        def unlist_step(group, carry):
            acc = list(carry)
            many = [group * 4 + u for u in range(4)]
            for half, (step_of, lane_of) in enumerate(((step0, lane0), (step1, lane1))):
                for f in range(FIELDS):
                    value = acc[2 * f + half]
                    for j in many:
                        row = jnp.broadcast_to(grad[j, pl.ds(f, 1), :], (8, LANES))
                        value = jnp.where(step_of == j + 1, take(row, lane_of), value)
                    acc[2 * f + half] = value
            return tuple(acc)

        acc = lax.fori_loop(0, quads, unlist_step, (jnp.zeros((8, LANES), F32),) * 18)
        for f in range(FIELDS):
            tab[f, pl.ds(tile_rows, 8), :] = acc[2 * f]
            tab[f, pl.ds(tile_rows + 8, 8), :] = acc[2 * f + 1]
        return carry

    lax.fori_loop(0, 16, tile_step, 0)
    errors = image_t[...] - target_t[...]
    total = jnp.sum(errors * errors, axis=0, keepdims=True)
    loss_ref[...] = jnp.broadcast_to(total, (128, LANES))
    for half in range(2):
        for k in range(FIELDS - 1):
            out_ref[pl.ds(k * 2 + half, 128, stride=MSG), :] = tab[
                k, half * 128 : half * 128 + 128, :
            ].T
        last_ref[pl.ds(half, 128, stride=2), :] = tab[
            FIELDS - 1, half * 128 : half * 128 + 128, :
        ].T
    for i in range(2):
        wide[:, i * 128 : i * 128 + 128] = image_t[i * 128 : i * 128 + 128, :].T
    image_ref[...] = wide[0:48, :]


def splat_back(
    width_px, height_px, cameras_ref, cos_ref, sin_ref,
    small_ref, harm_ref, ids_ref,
    ret_ref, ret_last_ref, losses_ref,
    gsmall_ref, gharm_ref, loss_ref,
    cams_ref, nat, by_row, stage,
):
    camera_numbers(cameras_ref, cos_ref, sin_ref, cams_ref)
    losses = jnp.sum(losses_ref[...], axis=0, keepdims=True)
    loss_ref[0, 0] = 0.5 * jnp.sum(losses)

    def clear_step(b, carry):
        by_row[pl.ds(pl.multiple_of(b * LANES + 8, 8), LANES), :] = jnp.zeros((LANES, LANES), F32)
        return carry

    lax.fori_loop(0, BLOCKS, clear_step, 0)

    def order_step(group, carry):
        for u in range(4):
            owner, half = slot_place(group * 4 + u)
            peers = [view * 32 + owner for view in range(VIEWS)]
            parts = [ret_ref[pl.ds(peer * MSG + half, 8, stride=2), :] for peer in peers]
            parts += [ret_last_ref[pl.ds(peer * 2 + half, 1), :] for peer in peers]
            parts.append(jnp.zeros((4, LANES), F32))
            stage[u, :, 0:TBL] = jnp.concatenate(parts, axis=0).T
        for u in range(4):
            for c in range(LANES):
                by_row[pl.ds(ids_ref[group * 4 + u, c] + 8, 1), :] = stage[u, c : c + 1, :]
        return carry

    lax.fori_loop(0, BLOCKS // 4, order_step, 0)

    def turn_step(group, carry):
        for u in range(4):
            n = group * 4 + u
            block = by_row[pl.ds(pl.multiple_of(n * LANES + 8, 8), LANES), 0:TBL].T
            for i in range(5):
                nat[pl.ds(8 * i * BLOCKS + n, 8, stride=BLOCKS), :] = block[8 * i : 8 * i + 8, :]
        return carry

    lax.fori_loop(0, BLOCKS // 4, turn_step, 0)

    def chunk_step(chunk, carry):
        centers, scales, rots, opacity = load_small(small_ref, chunk)

        def given(view, i):
            row = view * 8 + i if i < 8 else 32 + view
            return nat[pl.ds(pl.multiple_of(row * BLOCKS + chunk * 8, 8), 8), :]

        sigma, shape_pull = jax.vjp(shape_of, scales, rots)
        d_centers = [jnp.zeros((8, LANES), F32)] * 3
        d_sigma = [jnp.zeros((8, LANES), F32)] * 6
        d_opacity = jnp.zeros((8, LANES), F32)
        for view in range(VIEWS):
            cam = [cams_ref[view, i] for i in range(15)]
            _, geo_pull = jax.vjp(
                lambda c, s: geometry(c, s, cam, width_px, height_px), centers, sigma
            )
            d_c, d_s = geo_pull([given(view, i) for i in range(5)])
            basis, dir_pull = jax.vjp(lambda c: direction_basis(c, cam), centers)
            d_opacity = d_opacity + given(view, 5)
            d_basis = [jnp.zeros((8, LANES), F32)] * 16
            for colour in range(3):
                rows = [harm_slice(colour * 16 + i, chunk) for i in range(16)]
                coeffs = [harm_ref[row, :] for row in rows]
                total = sum(coeffs[i] * basis[i] for i in range(16)) + 0.5
                slope = jnp.where(total > 0.0, 1.0, jnp.where(total == 0.0, 0.5, 0.0))
                d_total = given(view, 6 + colour) * slope
                for i in range(16):
                    d_basis[i] = d_basis[i] + d_total * coeffs[i]
                    term = d_total * basis[i]
                    if view == 0:
                        gharm_ref[rows[i], :] = term
                    else:
                        gharm_ref[rows[i], :] = gharm_ref[rows[i], :] + term
            (d_dir,) = dir_pull(d_basis)
            d_centers = [d_centers[e] + d_c[e] + d_dir[e] for e in range(3)]
            d_sigma = [d_sigma[e] + d_s[e] for e in range(6)]
        d_scales, d_rots = shape_pull(d_sigma)
        values = list(d_centers) + list(d_scales) + list(d_rots)
        values.append(d_opacity * opacity * (1.0 - opacity))
        for i, value in enumerate(values):
            gsmall_ref[harm_slice(i, chunk), :] = value
        return carry

    lax.fori_loop(0, BLOCKS // 8, chunk_step, 0)


def tile_order(x):
    rows, width = x.shape
    split = x.reshape(rows // 8, 8, width // LANES, LANES)
    return split.transpose(0, 2, 1, 3).reshape(rows * width // LANES, LANES)


def from_tile_order(x, rows):
    width = x.shape[0] * LANES // rows
    split = x.reshape(rows // 8, width // LANES, 8, LANES)
    return split.transpose(0, 2, 1, 3).reshape(rows, width)


def params(mib):
    return pltpu.CompilerParams(vmem_limit_bytes=mib * 1024 * 1024)


def shape(*dims):
    return jax.ShapeDtypeStruct(dims, F32)


VM = functools.partial(pl.BlockSpec, memory_space=pltpu.VMEM)
SM = functools.partial(pl.BlockSpec, memory_space=pltpu.SMEM)


def exchange_kernel(count, *refs):
    sources, places = refs[:count], refs[count : 2 * count]
    sent, arrived, own = refs[2 * count :]
    view, pix = lax.axis_index("view"), lax.axis_index("pix")
    me = view * 32 + pix
    kept = [
        pltpu.make_async_copy(sources[i].at[me], places[i].at[me], own.at[i])
        for i in range(count)
    ]
    for copy in kept:
        copy.start()

    def send(step, carry):
        peer = lax.rem(me + step, 128)
        for i in range(count):
            pltpu.make_async_remote_copy(
                src_ref=sources[i].at[peer],
                dst_ref=places[i].at[me],
                send_sem=sent.at[i],
                recv_sem=arrived.at[i],
                device_id=(peer // 32, lax.rem(peer, 32)),
                device_id_type=pl.DeviceIdType.MESH,
            ).start()
        return carry

    lax.fori_loop(1, 128, send, 0)
    for copy in kept:
        copy.wait()
    for i in range(count):
        pltpu.make_async_remote_copy(
            src_ref=sources[i].at[pl.ds(0, 127)],
            dst_ref=places[i].at[pl.ds(0, 127)],
            send_sem=sent.at[i],
            recv_sem=arrived.at[i],
            device_id=(view, lax.rem(pix + 1, 32)),
            device_id_type=pl.DeviceIdType.MESH,
        ).wait()


def exchange(*messages):
    count = len(messages)
    blocks = [m.reshape(128, m.shape[0] // 128, LANES) for m in messages]
    outs = pl.pallas_call(
        functools.partial(exchange_kernel, count),
        out_shape=tuple(shape(*b.shape) for b in blocks),
        in_specs=[VM()] * count,
        out_specs=(VM(),) * count,
        scratch_shapes=[pltpu.SemaphoreType.DMA((count,))] * 3,
        compiler_params=pltpu.CompilerParams(
            has_side_effects=True, vmem_limit_bytes=16 * 1024 * 1024
        ),
        name="exchange",
    )(*blocks)
    return [out.reshape(m.shape) for out, m in zip(outs, messages)]


def local(
    centers, log_scales, rotations, logits, harmonic_coeffs,
    cameras, send_ids, tile_lists, tile_perm, targets,
):
    width_px = 16 * TW
    height_px = 16 * (512 // TW)
    views = (cameras, jnp.cos(cameras[:, :3]), jnp.sin(cameras[:, :3]))
    small = jnp.concatenate([centers, log_scales, rotations, logits[None]], axis=0)
    small = small.reshape(11, BLOCKS, LANES)
    harm = tile_order(harmonic_coeffs)
    ids = tile_order(send_ids[0])
    sending, sending_last = pl.pallas_call(
        functools.partial(splat_out, width_px, height_px),
        out_shape=(shape(128 * MSG, LANES), shape(256, LANES)),
        in_specs=[SM()] * 3 + [VM()] * 2 + [SM()],
        out_specs=(VM(), VM()),
        scratch_shapes=[
            pltpu.SMEM((VIEWS, 16), F32),
            pltpu.VMEM((BLOCKS * TBL, LANES), F32),
            pltpu.VMEM((BLOCKS * LANES + 8, LANES), F32),
            pltpu.VMEM((2, LANES, LANES), F32),
            pltpu.VMEM((2, LANES, LANES), F32),
        ],
        compiler_params=params(32),
        name="splat_out",
    )(*views, small, harm, ids)
    received = exchange(sending, sending_last)
    vreg = (8, LANES)
    *returning, image = pl.pallas_call(
        tiles,
        out_shape=(
            shape(128 * MSG, LANES), shape(256, LANES), shape(128, LANES), shape(48, 256),
        ),
        in_specs=[SM(), VM(), VM(), VM(), VM()],
        out_specs=(VM(), VM(), VM(), VM()),
        scratch_shapes=[
            pltpu.VMEM((FIELDS, 256, LANES), F32),
            pltpu.VMEM((LANES, 256), F32),
            pltpu.VMEM((256, LANES), F32),
            pltpu.VMEM((256, LANES), F32),
            pltpu.VMEM((16, 16, LANES), F32),
            pltpu.VMEM((16, 4) + vreg, F32),
            pltpu.VMEM((16, 32) + vreg, F32),
            pltpu.VMEM((16, 32) + vreg, F32),
            pltpu.VMEM((32,) + vreg, F32),
            pltpu.VMEM((3, 32) + vreg, F32),
            pltpu.VMEM((32,) + vreg, F32),
            pltpu.VMEM((3, 32) + vreg, F32),
            pltpu.VMEM((32,) + vreg, F32),
            pltpu.VMEM((16, 9) + vreg, F32),
            pltpu.VMEM((16, 16, LANES), F32),
            pltpu.VMEM((32, LANES), F32),
            pltpu.VMEM((3, 256, LANES), BF16),
        ],
        compiler_params=params(48),
        name="tiles",
    )(
        tile_perm,
        *received,
        tile_order(tile_lists),
        targets[0].transpose(1, 0, 2).reshape(48, 256),
    )
    returned = exchange(*returning)
    gsmall, gharm, total_loss = pl.pallas_call(
        functools.partial(splat_back, width_px, height_px),
        out_shape=(shape(16 * BLOCKS, LANES), shape(48 * BLOCKS, LANES), shape(1, 1)),
        in_specs=[SM()] * 3 + [VM()] * 2 + [SM()] + [VM()] * 3,
        out_specs=(VM(), VM(), SM()),
        scratch_shapes=[
            pltpu.SMEM((VIEWS, 16), F32),
            pltpu.VMEM((BLOCKS * TBL, LANES), F32),
            pltpu.VMEM((BLOCKS * LANES + 8, LANES), F32),
            pltpu.VMEM((4, LANES, LANES), F32),
        ],
        compiler_params=params(32),
        name="splat_back",
    )(*views, small, harm, ids, *returned)
    flat = from_tile_order(gsmall, 16)
    rendered = image.reshape(3, 16, 256).transpose(1, 0, 2)[None]
    return (
        rendered,
        total_loss[0, 0],
        flat[0:3],
        flat[3:6],
        flat[6:10],
        flat[10],
        from_tile_order(gharm, 48),
    )


def solution(mesh):
    both = ("view", "pix")
    return jax.shard_map(
        local,
        mesh=mesh,
        in_specs=(
            P(None, both),
            P(None, both),
            P(None, both),
            P(both),
            P(None, both),
            P(),
            P(both, None, None),
            P("pix", None),
            P("pix"),
            P("view", "pix", None, None),
        ),
        out_specs=(
            P("view", "pix", None, None),
            P(),
            P(None, both),
            P(None, both),
            P(None, both),
            P(both),
            P(None, both),
        ),
        check_vma=False,
    )
```
